256 devices in a mesh: dp: 128 (over x, y_hi, z, core), mp: 2 (over y_lo).
Axes of the slice: x: 4, y: 4 (y_hi: 2, y_lo: 2; y = y_hi * 2 + y_lo), z: 8, core: 2. Of those that a mesh axis runs over, the one named last changes fastest.
Arguments:
- picture_vectors: bfloat16 [131072, 1152], P('dp', 'mp'), may hold values from -5 to 5
- caption_vectors: bfloat16 [131072, 1152], P('dp', 'mp'), may hold values from -5 to 5
- sharpness_coefficient: float32 [1], replicated, may hold values from 4 to 8
- affinity_offset: float32 [1], replicated, may hold values from -4 to -2
Outputs:
- image_grad: float32 [131072, 1152], P('dp', 'mp')
- caption_vectors_derivative: float32 [131072, 1152], P('dp', 'mp')
- row_loss: float32 [131072], P(('dp', 'mp'))
The draws below stay inside these ranges and needn't reach their ends.
All inputs are finite; a program needn't handle non-finite values.
Results may differ from the reference program's by a relative error of at most 0.0045.
Values may be sent and summed in bfloat16 or wider, within the bound.
A program may use at most 128 MiB of HBM per device.

```python
import math
import jax
import jax.numpy as jnp
from jax import lax

D = 1152
ROWS = 1024
TOKENS = 131072
N_DP = 128


def shared_pairs(key):
    return jax.random.normal(key, (TOKENS, D), jnp.float32)


def finish_draw(shared_base, noise_part, random_seed_for_columns, key_row, row_ceiling):
    column_scale = jnp.exp(math.log(3.0) * jnp.arange(D, dtype=jnp.float32) / D + math.log(3.3) * jax.random.uniform(random_seed_for_columns, (D,), jnp.float32))
    row_scale = jnp.exp(jax.random.uniform(key_row, (TOKENS, 1), jnp.float32) * math.log(row_ceiling))
    values = (shared_base + noise_part) * column_scale[None, :] * row_scale
    values = values * (0.25 / math.sqrt(D * 22.0))
    return values.astype(jnp.bfloat16)


def draw_picture_vectors(key, part):
    shared_base = shared_pairs(key)
    key = jax.random.fold_in(key, 11)
    random_seed_for_columns, key_noise, key_row = jax.random.split(key, 3)
    noise_part = jax.random.normal(key_noise, (TOKENS, D), jnp.float32)
    return finish_draw(shared_base, noise_part, random_seed_for_columns, key_row, 10.0)


def draw_caption_vectors(key, part):
    shared_base = shared_pairs(key)
    key = jax.random.fold_in(key, 23)
    random_seed_for_columns, key_noise, key_row = jax.random.split(key, 3)
    noise_part = jax.random.normal(key_noise, (TOKENS, D), jnp.float32)
    return finish_draw(shared_base, noise_part, random_seed_for_columns, key_row, 10.0)


def setup_inputs(seed: int = 0) -> dict:
    keys = jax.random.split(jax.random.key(seed), 5)
    picture_vectors = draw_picture_vectors(jax.random.fold_in(keys[4], 71), 0)
    caption_vectors = draw_caption_vectors(jax.random.fold_in(keys[4], 71), 0)
    sharpness_coefficient = jnp.clip(jax.random.uniform(keys[2], (1,), jnp.float32, 4.0, 8.0), 4.0, 8.0)
    affinity_offset = jnp.clip(jax.random.uniform(keys[3], (1,), jnp.float32, -4.0, -2.0), -4.0, -2.0)
    return dict(picture_vectors=picture_vectors, caption_vectors=caption_vectors, sharpness_coefficient=sharpness_coefficient, affinity_offset=affinity_offset)


epsilon = 1e-06

def reference(picture_vectors, caption_vectors, sharpness_coefficient, affinity_offset):
    image_float = picture_vectors.astype(jnp.float32)
    text_float = caption_vectors.astype(jnp.float32)
    image_inverse = lax.rsqrt(lax.optimization_barrier(jnp.sum(image_float * image_float, axis=1)) + epsilon)
    text_inverse = lax.rsqrt(lax.optimization_barrier(jnp.sum(text_float * text_float, axis=1)) + epsilon)
    image_unit = (image_float * image_inverse[:, None]).astype(jnp.bfloat16)
    text_unit = (text_float * text_inverse[:, None]).astype(jnp.bfloat16)
    text_previous = jnp.roll(text_unit, ROWS, axis=0)
    multiplier_amount = sharpness_coefficient[0]
    block_shift = affinity_offset[0]
    blocks_in = (image_unit.reshape(N_DP, ROWS, D), text_unit.reshape(N_DP, ROWS, D), text_previous.reshape(N_DP, ROWS, D))

    def group_terms(block_args):
        image_batch_rows, text_batch_rows, preceding_text_rows = block_args
        local_logit_block = multiplier_amount * jnp.dot(image_batch_rows, text_batch_rows.T, preferred_element_type=jnp.float32) + block_shift
        preceding_logit_block = multiplier_amount * jnp.dot(image_batch_rows, preceding_text_rows.T, preferred_element_type=jnp.float32) + block_shift
        row_index = lax.broadcasted_iota(jnp.int32, (ROWS, ROWS), 0)
        col_index = lax.broadcasted_iota(jnp.int32, (ROWS, ROWS), 1)
        local_label_sign = jnp.where(row_index == col_index, jnp.float32(1.0), jnp.float32(-1.0))
        losses = (lax.optimization_barrier(jnp.sum(jax.nn.softplus(-local_label_sign * local_logit_block), axis=1)) + lax.optimization_barrier(jnp.sum(jax.nn.softplus(preceding_logit_block), axis=1))) / (2 * ROWS)
        local_block_weight = (multiplier_amount * -local_label_sign * jax.nn.sigmoid(-local_label_sign * local_logit_block)).astype(jnp.bfloat16)
        preceding_block_weight = (multiplier_amount * jax.nn.sigmoid(preceding_logit_block)).astype(jnp.bfloat16)
        image_partial = jnp.dot(local_block_weight, text_batch_rows, preferred_element_type=jnp.float32) + jnp.dot(preceding_block_weight, preceding_text_rows, preferred_element_type=jnp.float32)
        text_own = jnp.dot(local_block_weight.T, image_batch_rows, preferred_element_type=jnp.float32)
        text_far = jnp.dot(preceding_block_weight.T, image_batch_rows, preferred_element_type=jnp.float32)
        return (losses, image_partial, text_own, text_far)
    losses, image_partial, text_own, text_far = lax.map(group_terms, blocks_in)
    row_loss = losses.reshape(TOKENS)
    image_partial = image_partial.reshape(TOKENS, D)
    text_total = text_own.reshape(TOKENS, D) + jnp.roll(text_far.reshape(TOKENS, D), -ROWS, axis=0)
    image_back = image_unit.astype(jnp.float32)
    text_back = text_unit.astype(jnp.float32)
    image_dot = lax.optimization_barrier(jnp.sum(image_back * image_partial, axis=1))
    text_dot = lax.optimization_barrier(jnp.sum(text_back * text_total, axis=1))
    image_grad = (image_partial - image_back * image_dot[:, None]) * image_inverse[:, None]
    caption_vectors_derivative = (text_total - text_back * text_dot[:, None]) * text_inverse[:, None]
    return (image_grad, caption_vectors_derivative, row_loss)
```

```python
import functools

import jax
import jax.numpy as jnp
from jax import lax
from jax.experimental import pallas as pl
from jax.experimental.pallas import tpu as pltpu
from jax.sharding import PartitionSpec as P

MESH = pl.DeviceIdType.MESH
F32 = jnp.float32
BF16 = jnp.bfloat16
EPSILON = 1e-06
LOG2E = 1.4426950408889634
TURN = 16
TILE_ROWS = 512
CHUNK = 256


def kernel(
    image,
    text,
    sharpness,
    offset,
    image_out,
    text_out,
    loss_out,
    image_raw,
    text_raw,
    image_unit,
    image_rows,
    text_unit,
    image_acc,
    text_acc,
    far_send,
    far_recv,
    dots,
    far_dots,
    row_dots,
    products,
    logs,
    image_inverse,
    text_inverse,
    image_ss,
    image_rs,
    text_ss,
    text_rs,
    whole_ss,
    whole_rs,
    pass_ss,
    pass_rs,
    far_ss,
    far_rs,
    dot_ss,
    dot_rs,
    local_sem,
    out_sem,
    go_sem,
):
    half, rows = image.shape
    chunks = rows // CHUNK
    halves = rows // TILE_ROWS
    blocks = lax.axis_size("dp")
    dp = lax.axis_index("dp")
    mp = lax.axis_index("mp")
    core = lax.rem(dp, 2)
    turn_next = (lax.rem(dp, TURN) == TURN - 1).astype(jnp.int32)
    turn_prev = (lax.rem(dp, TURN) == 0).astype(jnp.int32)
    partner = (dp, 1 - mp)
    following = (lax.rem(dp + 1, blocks), mp + turn_next * (1 - 2 * mp))
    preceding = (lax.rem(dp + blocks - 1, blocks), mp + turn_prev * (1 - 2 * mp))
    own_slot = 1 - core
    prev_slot = core
    prev_offset = pl.multiple_of(turn_prev * half, half)

    def span(start, size):
        return pl.ds(pl.multiple_of(start, size), size)

    def columns(j):
        return span(j * CHUNK, CHUNK)

    def remote(src, dst, send, recv, device):
        return pltpu.make_async_remote_copy(
            src_ref=src,
            dst_ref=dst,
            send_sem=send,
            recv_sem=recv,
            device_id=device,
            device_id_type=MESH,
        )

    def image_copy(j):
        return remote(
            image.at[:, columns(j)],
            image_raw.at[pl.ds(half, half), columns(j)],
            image_ss.at[j],
            image_rs.at[j],
            partner,
        )

    def text_copy(j):
        return remote(
            text.at[:, columns(j)],
            text_raw.at[own_slot, pl.ds(half, half), columns(j)],
            text_ss.at[j],
            text_rs.at[j],
            partner,
        )

    def whole_copy(slot, turned):
        return remote(
            text,
            text_raw.at[slot, span(turned * half, half), :],
            whole_ss.at[0],
            whole_rs.at[0],
            following,
        )

    def pass_copy(slot, turned, j):
        return remote(
            text_raw.at[own_slot, pl.ds(half, half), columns(j)],
            text_raw.at[slot, span((1 - turned) * half, half), columns(j)],
            pass_ss.at[j],
            pass_rs.at[j],
            following,
        )

    def far_copy(j):
        return remote(
            far_send.at[:, columns(j)],
            far_recv.at[:, columns(j)],
            far_ss.at[j],
            far_rs.at[j],
            preceding,
        )

    def dot_copy(j):
        return remote(
            dots.at[prev_slot, :, columns(j)],
            far_dots.at[:, columns(j)],
            dot_ss.at[j],
            dot_rs.at[j],
            preceding,
        )

    def image_here():
        return pltpu.make_async_copy(image, image_raw.at[pl.ds(0, half), :], local_sem.at[0])

    def text_here():
        return pltpu.make_async_copy(
            text, text_raw.at[own_slot, pl.ds(0, half), :], local_sem.at[1]
        )

    def image_result(j):
        return pltpu.make_async_copy(
            image_acc.at[:, columns(j)], image_out.at[:, columns(j)], out_sem.at[0, j]
        )

    def text_result(j):
        return pltpu.make_async_copy(
            text_acc.at[own_slot, :, columns(j)], text_out.at[:, columns(j)], out_sem.at[1, j]
        )

    def each(count, body):
        def step(j, carry):
            body(j)
            return carry

        lax.fori_loop(0, count, step, 0)

    scale = sharpness[0]
    slope = scale * LOG2E
    shift = offset[0] * LOG2E

    def normal(raw):
        values = raw.astype(F32)
        inverse = lax.rsqrt(jnp.sum(values * values, axis=0, keepdims=True) + EPSILON)
        return (values * inverse).astype(BF16), inverse

    def prepare_text(slot, j):
        unit, inverse = normal(text_raw[slot, :, columns(j)])
        text_unit[slot, :, columns(j)] = unit
        text_inverse[slot, 0:1, columns(j)] = inverse

    def prepare_image(j):
        unit, inverse = normal(image_raw[:, columns(j)])
        image_unit[:, columns(j)] = unit
        image_inverse[0:1, columns(j)] = inverse
        image_rows[columns(j), :] = unit.T

    def tile(slot, own, h, j, place):
        here = span(h * TILE_ROWS, TILE_ROWS)
        there = columns(j)
        dot = jnp.dot(image_rows[here, :], text_unit[slot, :, there], preferred_element_type=F32)
        power = dot * slope + shift
        if own:
            row = lax.broadcasted_iota(jnp.int32, dot.shape, 0) + h * TILE_ROWS
            column = lax.broadcasted_iota(jnp.int32, dot.shape, 1) + j * CHUNK
            paired = row == column
            power = jnp.where(paired, -power, power)
        term = jnp.exp2(power)
        total = term + 1.0
        weight = (term * scale) / total
        if own:
            weight = jnp.where(paired, -weight, weight)
        product = weight * dot
        row_dots[here, :] += product[:, :128] + product[:, 128:]
        products[here, :] *= total[:, :128] * total[:, 128:]
        dots[slot, 0:1, there] += jnp.sum(product, axis=0, keepdims=True)
        rounded = weight.astype(BF16)
        image_acc[:, here] += lax.dot_general(
            text_unit[slot, pl.ds(0, half), there],
            rounded,
            (((1,), (1,)), ((), ())),
            preferred_element_type=F32,
        )
        text_acc[slot, :, there] += jnp.dot(
            image_unit[pl.ds(place, half), here], rounded, preferred_element_type=F32
        )

    def take_logs():
        logs[...] += jnp.log(products[...])
        products[...] = jnp.ones_like(products)

    def send_far(slot, j):
        far_send[:, columns(j)] = text_acc[slot, :, columns(j)].astype(BF16)
        far_copy(j).start()
        dot_copy(j).start()

    def finish_image():
        image_dot = jnp.sum(row_dots[...].T, axis=0, keepdims=True)
        for j in range(chunks):
            cut = slice(j * CHUNK, (j + 1) * CHUNK)
            back = image_unit[0:half, cut].astype(F32)
            image_acc[:, cut] = (image_acc[:, cut] - back * image_dot[:, cut]) * image_inverse[
                0:1, cut
            ]
            image_result(j).start()

    def finish_loss():
        take_logs()
        image_inverse[0:1, :] = jnp.sum(logs[...].T, axis=0, keepdims=True) / (2 * rows)
        share = rows // 2
        loss_out[...] = image_inverse[0:1, span(mp * share, share)]

    def finish_text(slot, j):
        cut = columns(j)
        far_copy(j).wait_recv()
        dot_copy(j).wait_recv()
        total = text_acc[slot, :, cut] + far_recv[:, cut].astype(F32)
        dot = dots[slot, 0:1, cut] + far_dots[0:1, cut]
        back = text_unit[slot, pl.ds(0, half), cut].astype(F32)
        text_acc[slot, :, cut] = (total - back * dot) * text_inverse[slot, 0:1, cut]
        text_result(j).start()

    image_here().start()
    text_here().start()
    barrier = pltpu.get_barrier_semaphore()
    for device in (partner, following, preceding):
        pl.semaphore_signal(barrier, inc=1, device_id=device, device_id_type=MESH)
    pl.semaphore_wait(barrier, 3)

    @pl.when(core == 0)
    def _():
        each(chunks, lambda j: image_copy(j).start())

    @pl.when(core == 1)
    def _():
        each(chunks, lambda j: text_copy(j).start())
        each(chunks, lambda j: image_copy(j).start())

    whole_copy(own_slot, turn_next).start()

    image_acc[...] = jnp.zeros_like(image_acc)
    text_acc[...] = jnp.zeros_like(text_acc)
    dots[...] = jnp.zeros_like(dots)
    row_dots[...] = jnp.zeros_like(row_dots)
    logs[...] = jnp.zeros_like(logs)
    products[...] = jnp.ones_like(products)
    image_here().wait()
    text_here().wait()

    @pl.when(core == 0)
    def _():
        whole_copy(prev_slot, turn_prev).wait_recv()

        def ready(j):
            pass_copy(prev_slot, turn_prev, j).wait_recv()
            prepare_text(0, j)
            image_copy(j).wait_recv()
            prepare_image(j)

        each(chunks, ready)

        def first(j):
            each(halves, lambda h: tile(0, False, h, j, prev_offset))
            send_far(0, j)

        each(chunks, first)
        pl.semaphore_wait(go_sem, 1)
        each(chunks, lambda j: text_copy(j).start())
        take_logs()

        def second(j):
            text_copy(j).wait_recv()
            pass_copy(own_slot, turn_next, j).start()
            prepare_text(1, j)
            each(halves, lambda h: tile(1, True, h, j, 0))

        each(chunks, second)
        finish_image()
        finish_loss()
        each(chunks, lambda j: finish_text(1, j))

    @pl.when(core == 1)
    def _():
        def ready(j):
            text_copy(j).wait_recv()
            pass_copy(own_slot, turn_next, j).start()
            prepare_text(0, j)

        each(chunks, ready)

        per_half = TILE_ROWS // CHUNK

        def first(h):
            def arrive(i):
                image_copy(h * per_half + i).wait_recv()
                prepare_image(h * per_half + i)

            each(per_half, arrive)
            image_copy(h * per_half).wait_send()

            @pl.when(h == halves - 1)
            def _():
                pl.semaphore_signal(go_sem, inc=1, device_id=preceding, device_id_type=MESH)

            each(chunks, lambda j: tile(0, True, h, j, 0))

        each(halves, first)
        take_logs()
        whole_copy(prev_slot, turn_prev).wait_recv()

        def second(j):
            pass_copy(prev_slot, turn_prev, j).wait_recv()
            prepare_text(1, j)
            each(halves, lambda h: tile(1, False, h, j, 0))
            send_far(1, j)

        each(chunks, second)
        each(chunks, lambda j: finish_text(0, j))
        finish_image()
        finish_loss()

    def settle(j):
        text_copy(j).wait_send()
        pass_copy(own_slot, turn_next, j).wait_send()
        far_copy(j).wait_send()
        dot_copy(j).wait_send()
        image_result(j).wait()
        text_result(j).wait()

    each(chunks, settle)
    whole_copy(own_slot, turn_next).wait_send()

    @pl.when(core == 0)
    def _():
        each(chunks, lambda j: image_copy(j).wait_send())

    @pl.when(core == 1)
    def _():
        per_half = TILE_ROWS // CHUNK

        def rest(j):
            @pl.when(lax.rem(j, per_half) != 0)
            def _():
                image_copy(j).wait_send()

        each(chunks, rest)


def per_device(picture_vectors, caption_vectors, sharpness_coefficient, affinity_offset):
    rows, half = picture_vectors.shape
    chunks = rows // CHUNK
    width = 2 * half
    anywhere = pl.BlockSpec(memory_space=pl.ANY)
    scalar = pl.BlockSpec(memory_space=pltpu.SMEM)
    dma = pltpu.SemaphoreType.DMA
    image_grad, text_grad, row_loss = pl.pallas_call(
        kernel,
        out_shape=(
            jax.ShapeDtypeStruct((half, rows), F32),
            jax.ShapeDtypeStruct((half, rows), F32),
            jax.ShapeDtypeStruct((1, rows // 2), F32),
        ),
        in_specs=[anywhere, anywhere, scalar, scalar],
        out_specs=(anywhere, anywhere, pl.BlockSpec(memory_space=pltpu.VMEM)),
        scratch_shapes=[
            pltpu.VMEM((width, rows), BF16),
            pltpu.VMEM((2, width, rows), BF16),
            pltpu.VMEM((width, rows), BF16),
            pltpu.VMEM((rows, width), BF16),
            pltpu.VMEM((2, width, rows), BF16),
            pltpu.VMEM((half, rows), F32),
            pltpu.VMEM((2, half, rows), F32),
            pltpu.VMEM((half, rows), BF16),
            pltpu.VMEM((half, rows), BF16),
            pltpu.VMEM((2, 8, rows), F32),
            pltpu.VMEM((8, rows), F32),
            pltpu.VMEM((rows, 128), F32),
            pltpu.VMEM((rows, 128), F32),
            pltpu.VMEM((rows, 128), F32),
            pltpu.VMEM((8, rows), F32),
            pltpu.VMEM((2, 8, rows), F32),
            dma((chunks,)),
            dma((chunks,)),
            dma((chunks,)),
            dma((chunks,)),
            dma((1,)),
            dma((1,)),
            dma((chunks,)),
            dma((chunks,)),
            dma((chunks,)),
            dma((chunks,)),
            dma((chunks,)),
            dma((chunks,)),
            dma((2,)),
            dma((2, chunks)),
            pltpu.SemaphoreType.REGULAR,
        ],
        compiler_params=pltpu.CompilerParams(
            collective_id=0, has_side_effects=True, vmem_limit_bytes=48 * 1024 * 1024
        ),
        cost_estimate=pl.CostEstimate(
            flops=8 * rows * rows * width, bytes_accessed=12 * half * rows, transcendentals=0
        ),
    )(picture_vectors.T, caption_vectors.T, sharpness_coefficient, affinity_offset)
    return image_grad.T, text_grad.T, row_loss.reshape(rows // 2)


def solution(mesh):
    placed = (P("dp", "mp"), P("dp", "mp"), P(), P())
    return jax.shard_map(
        per_device,
        mesh=mesh,
        in_specs=placed,
        out_specs=(P("dp", "mp"), P("dp", "mp"), P(("dp", "mp"))),
        check_vma=False,
    )
```

```python
import functools

import jax
import jax.numpy as jnp
from jax import lax
from jax.experimental import pallas as pl
from jax.experimental.pallas import tpu as pltpu
from jax.sharding import PartitionSpec as P

MESH = pl.DeviceIdType.MESH
F32 = jnp.float32
BF16 = jnp.bfloat16
EPSILON = 1e-06
LOG2E = 1.4426950408889634
TURN = 16
TILE_ROWS = 512
CHUNK = 256
SMALL_PARTS = 4


def kernel(
    image,
    text,
    sharpness,
    offset,
    image_out,
    text_out,
    loss_out,
    image_raw,
    text_raw,
    image_unit,
    image_rows,
    text_unit,
    image_acc,
    text_acc,
    far_send,
    far_recv,
    dots,
    far_dots,
    row_dots,
    products,
    logs,
    image_inverse,
    text_inverse,
    image_ss,
    image_rs,
    text_ss,
    text_rs,
    whole_ss,
    whole_rs,
    pass_ss,
    pass_rs,
    far_ss,
    far_rs,
    dot_ss,
    dot_rs,
    local_sem,
    out_sem,
    go_sem,
):
    half, rows = image.shape
    chunks = rows // CHUNK
    halves = rows // TILE_ROWS
    blocks = lax.axis_size("dp")
    dp = lax.axis_index("dp")
    mp = lax.axis_index("mp")
    core = lax.rem(dp, 2)
    turn_next = (lax.rem(dp, TURN) == TURN - 1).astype(jnp.int32)
    turn_prev = (lax.rem(dp, TURN) == 0).astype(jnp.int32)
    partner = (dp, 1 - mp)
    following = (lax.rem(dp + 1, blocks), mp + turn_next * (1 - 2 * mp))
    preceding = (lax.rem(dp + blocks - 1, blocks), mp + turn_prev * (1 - 2 * mp))
    own_slot = 1 - core
    prev_slot = core
    prev_offset = pl.multiple_of(turn_prev * half, half)

    def span(start, size):
        return pl.ds(pl.multiple_of(start, size), size)

    def columns(j):
        return span(j * CHUNK, CHUNK)

    def remote(src, dst, send, recv, device):
        return pltpu.make_async_remote_copy(
            src_ref=src,
            dst_ref=dst,
            send_sem=send,
            recv_sem=recv,
            device_id=device,
            device_id_type=MESH,
        )

    def image_copy(j):
        return remote(
            image.at[:, columns(j)],
            image_raw.at[pl.ds(half, half), columns(j)],
            image_ss.at[j],
            image_rs.at[j],
            partner,
        )

    def text_copy(j):
        return remote(
            text.at[:, columns(j)],
            text_raw.at[own_slot, pl.ds(half, half), columns(j)],
            text_ss.at[j],
            text_rs.at[j],
            partner,
        )

    def whole_copy(slot, turned):
        return remote(
            text,
            text_raw.at[slot, span(turned * half, half), :],
            whole_ss.at[0],
            whole_rs.at[0],
            following,
        )

    def pass_copy(slot, turned, j):
        return remote(
            text_raw.at[own_slot, pl.ds(half, half), columns(j)],
            text_raw.at[slot, span((1 - turned) * half, half), columns(j)],
            pass_ss.at[j],
            pass_rs.at[j],
            following,
        )

    def far_copy(j):
        return remote(
            far_send.at[:, columns(j)],
            far_recv.at[:, columns(j)],
            far_ss.at[j],
            far_rs.at[j],
            preceding,
        )

    def dot_copy(j):
        return remote(
            dots.at[prev_slot, :, columns(j)],
            far_dots.at[:, columns(j)],
            dot_ss.at[j],
            dot_rs.at[j],
            preceding,
        )

    def image_here():
        return pltpu.make_async_copy(image, image_raw.at[pl.ds(0, half), :], local_sem.at[0])

    def text_here():
        return pltpu.make_async_copy(
            text, text_raw.at[own_slot, pl.ds(0, half), :], local_sem.at[1]
        )

    def image_result(j):
        return pltpu.make_async_copy(
            image_acc.at[:, columns(j)], image_out.at[:, columns(j)], out_sem.at[0, j]
        )

    def text_result(j):
        return pltpu.make_async_copy(
            text_acc.at[own_slot, :, columns(j)], text_out.at[:, columns(j)], out_sem.at[1, j]
        )

    def each(count, body):
        def step(j, carry):
            body(j)
            return carry

        lax.fori_loop(0, count, step, 0)

    scale = sharpness[0]
    slope = scale * LOG2E
    shift = offset[0] * LOG2E

    def normal(raw):
        values = raw.astype(F32)
        inverse = lax.rsqrt(jnp.sum(values * values, axis=0, keepdims=True) + EPSILON)
        return (values * inverse).astype(BF16), inverse

    def prepare_text(slot, j):
        unit, inverse = normal(text_raw[slot, :, columns(j)])
        text_unit[slot, :, columns(j)] = unit
        text_inverse[slot, 0:1, columns(j)] = inverse

    def prepare_image(j):
        unit, inverse = normal(image_raw[:, columns(j)])
        image_unit[:, columns(j)] = unit
        image_inverse[0:1, columns(j)] = inverse
        image_rows[columns(j), :] = unit.T

    def tile(slot, own, row, height, column, width, place, parts=1):
        there = pl.ds(pl.multiple_of(column, CHUNK), width)
        size = height // parts
        spans = [pl.ds(pl.multiple_of(row + i * size, size), size) for i in range(parts)]
        scores = [
            jnp.dot(image_rows[here, :], text_unit[slot, :, there], preferred_element_type=F32)
            for here in spans
        ]
        grads = []
        inner = jnp.zeros((1, width), F32)
        for i, (here, dot) in enumerate(zip(spans, scores)):
            power = dot * slope + shift
            if own:
                first = lax.broadcasted_iota(jnp.int32, dot.shape, 0) + (row + i * size - column)
                paired = first == lax.broadcasted_iota(jnp.int32, dot.shape, 1)
                power = jnp.where(paired, -power, power)
            term = jnp.exp2(power)
            total = term + 1.0
            weight = (term * scale) / total
            if own:
                weight = jnp.where(paired, -weight, weight)
            product = weight * dot
            summed, multiplied = product[:, :128], total[:, :128]
            for lane in range(128, width, 128):
                summed += product[:, lane : lane + 128]
                multiplied *= total[:, lane : lane + 128]
            row_dots[here, :] += summed
            products[here, :] *= multiplied
            inner += jnp.sum(product, axis=0, keepdims=True)
            rounded = weight.astype(BF16)
            image_acc[:, here] += lax.dot_general(
                text_unit[slot, pl.ds(0, half), there],
                rounded,
                (((1,), (1,)), ((), ())),
                preferred_element_type=F32,
            )
            grads.append(
                jnp.dot(image_unit[pl.ds(place, half), here], rounded, preferred_element_type=F32)
            )
        dots[slot, 0:1, there] += inner
        text_acc[slot, :, there] += sum(grads[1:], grads[0])

    def take_logs():
        logs[...] += jnp.log(products[...])
        products[...] = jnp.ones_like(products)

    def send_far(slot, j):
        far_send[:, columns(j)] = text_acc[slot, :, columns(j)].astype(BF16)
        far_copy(j).start()
        dot_copy(j).start()

    def finish_image():
        image_dot = jnp.sum(row_dots[...].T, axis=0, keepdims=True)
        for j in range(chunks):
            cut = slice(j * CHUNK, (j + 1) * CHUNK)
            back = image_unit[0:half, cut].astype(F32)
            image_acc[:, cut] = (image_acc[:, cut] - back * image_dot[:, cut]) * image_inverse[
                0:1, cut
            ]
            image_result(j).start()

    def finish_loss():
        take_logs()
        image_inverse[0:1, :] = jnp.sum(logs[...].T, axis=0, keepdims=True) / (2 * rows)
        share = rows // 2
        loss_out[...] = image_inverse[0:1, span(mp * share, share)]

    def finish_text(slot, j):
        cut = columns(j)
        far_copy(j).wait_recv()
        dot_copy(j).wait_recv()
        total = text_acc[slot, :, cut] + far_recv[:, cut].astype(F32)
        dot = dots[slot, 0:1, cut] + far_dots[0:1, cut]
        back = text_unit[slot, pl.ds(0, half), cut].astype(F32)
        text_acc[slot, :, cut] = (total - back * dot) * text_inverse[slot, 0:1, cut]
        text_result(j).start()

    image_here().start()
    text_here().start()
    barrier = pltpu.get_barrier_semaphore()
    for device in (partner, following, preceding):
        pl.semaphore_signal(barrier, inc=1, device_id=device, device_id_type=MESH)
    pl.semaphore_wait(barrier, 3)

    @pl.when(core == 0)
    def _():
        each(chunks, lambda j: image_copy(j).start())

    @pl.when(core == 1)
    def _():
        each(chunks, lambda j: text_copy(j).start())
        each(chunks, lambda j: image_copy(j).start())

    whole_copy(own_slot, turn_next).start()

    image_acc[...] = jnp.zeros_like(image_acc)
    text_acc[...] = jnp.zeros_like(text_acc)
    dots[...] = jnp.zeros_like(dots)
    row_dots[...] = jnp.zeros_like(row_dots)
    logs[...] = jnp.zeros_like(logs)
    products[...] = jnp.ones_like(products)
    image_here().wait()
    text_here().wait()

    @pl.when(core == 0)
    def _():
        def arrive(j):
            image_copy(j).wait_recv()
            prepare_image(j)

        each(chunks, arrive)
        whole_copy(prev_slot, turn_prev).wait_recv()

        def first(i):
            def ready(j):
                pass_copy(prev_slot, turn_prev, 2 * i + j).wait_recv()
                prepare_text(0, 2 * i + j)

            each(2, ready)
            tile(0, False, 0, rows, 2 * i * CHUNK, 2 * CHUNK, prev_offset)
            each(2, lambda j: send_far(0, 2 * i + j))

        each(chunks // 2, first)
        pl.semaphore_wait(go_sem, 1)
        each(chunks, lambda j: text_copy(j).start())
        take_logs()

        def ready(j):
            text_copy(j).wait_recv()
            pass_copy(own_slot, turn_next, j).start()
            prepare_text(1, j)

        each(2, ready)
        tile(1, True, 0, rows, 0, 2 * CHUNK, 0)

        def second(j):
            ready(j + 2)
            tile(1, True, 0, rows, (j + 2) * CHUNK, CHUNK, 0, SMALL_PARTS)

        each(chunks - 2, second)
        finish_image()
        finish_loss()
        each(chunks, lambda j: finish_text(1, j))

    @pl.when(core == 1)
    def _():
        def ready(j):
            text_copy(j).wait_recv()
            pass_copy(own_slot, turn_next, j).start()
            prepare_text(0, j)

        each(chunks, ready)

        per_half = TILE_ROWS // CHUNK

        def first(h):
            def arrive(i):
                image_copy(h * per_half + i).wait_recv()
                prepare_image(h * per_half + i)

            each(per_half, arrive)
            image_copy(h * per_half).wait_send()

            @pl.when(h == halves - 1)
            def _():
                pl.semaphore_signal(go_sem, inc=1, device_id=preceding, device_id_type=MESH)

            each(
                2,
                lambda i: tile(0, True, h * TILE_ROWS, TILE_ROWS, 2 * i * CHUNK, 2 * CHUNK, 0),
            )

        each(halves, first)
        take_logs()
        whole_copy(prev_slot, turn_prev).wait_recv()

        def come(j):
            pass_copy(prev_slot, turn_prev, j).wait_recv()
            prepare_text(1, j)

        each(2, come)
        tile(1, False, 0, rows, 0, 2 * CHUNK, 0)
        each(2, lambda j: send_far(1, j))

        def second(j):
            come(j + 2)
            tile(1, False, 0, rows, (j + 2) * CHUNK, CHUNK, 0, SMALL_PARTS)
            send_far(1, j + 2)

        each(chunks - 2, second)
        each(chunks, lambda j: finish_text(0, j))
        finish_image()
        finish_loss()

    def settle(j):
        text_copy(j).wait_send()
        pass_copy(own_slot, turn_next, j).wait_send()
        far_copy(j).wait_send()
        dot_copy(j).wait_send()
        image_result(j).wait()
        text_result(j).wait()

    each(chunks, settle)
    whole_copy(own_slot, turn_next).wait_send()

    @pl.when(core == 0)
    def _():
        each(chunks, lambda j: image_copy(j).wait_send())

    @pl.when(core == 1)
    def _():
        per_half = TILE_ROWS // CHUNK

        def rest(j):
            @pl.when(lax.rem(j, per_half) != 0)
            def _():
                image_copy(j).wait_send()

        each(chunks, rest)


def per_device(picture_vectors, caption_vectors, sharpness_coefficient, affinity_offset):
    rows, half = picture_vectors.shape
    chunks = rows // CHUNK
    width = 2 * half
    anywhere = pl.BlockSpec(memory_space=pl.ANY)
    held = pl.BlockSpec(memory_space=pltpu.HBM)
    scalar = pl.BlockSpec(memory_space=pltpu.SMEM)
    dma = pltpu.SemaphoreType.DMA
    image_grad, text_grad, row_loss = pl.pallas_call(
        kernel,
        out_shape=(
            jax.ShapeDtypeStruct((half, rows), F32),
            jax.ShapeDtypeStruct((half, rows), F32),
            jax.ShapeDtypeStruct((1, rows // 2), F32),
        ),
        in_specs=[held, held, scalar, scalar],
        out_specs=(anywhere, anywhere, pl.BlockSpec(memory_space=pltpu.VMEM)),
        scratch_shapes=[
            pltpu.VMEM((width, rows), BF16),
            pltpu.VMEM((2, width, rows), BF16),
            pltpu.VMEM((width, rows), BF16),
            pltpu.VMEM((rows, width), BF16),
            pltpu.VMEM((2, width, rows), BF16),
            pltpu.VMEM((half, rows), F32),
            pltpu.VMEM((2, half, rows), F32),
            pltpu.VMEM((half, rows), BF16),
            pltpu.VMEM((half, rows), BF16),
            pltpu.VMEM((2, 8, rows), F32),
            pltpu.VMEM((8, rows), F32),
            pltpu.VMEM((rows, 128), F32),
            pltpu.VMEM((rows, 128), F32),
            pltpu.VMEM((rows, 128), F32),
            pltpu.VMEM((8, rows), F32),
            pltpu.VMEM((2, 8, rows), F32),
            dma((chunks,)),
            dma((chunks,)),
            dma((chunks,)),
            dma((chunks,)),
            dma((1,)),
            dma((1,)),
            dma((chunks,)),
            dma((chunks,)),
            dma((chunks,)),
            dma((chunks,)),
            dma((chunks,)),
            dma((chunks,)),
            dma((2,)),
            dma((2, chunks)),
            pltpu.SemaphoreType.REGULAR,
        ],
        compiler_params=pltpu.CompilerParams(
            collective_id=0, has_side_effects=True, vmem_limit_bytes=60 * 1024 * 1024
        ),
        cost_estimate=pl.CostEstimate(
            flops=8 * rows * rows * width, bytes_accessed=12 * half * rows, transcendentals=0
        ),
    )(picture_vectors.T, caption_vectors.T, sharpness_coefficient, affinity_offset)
    return image_grad.T, text_grad.T, row_loss.reshape(rows // 2)


def solution(mesh):
    placed = (P("dp", "mp"), P("dp", "mp"), P(), P())
    return jax.shard_map(
        per_device,
        mesh=mesh,
        in_specs=placed,
        out_specs=(P("dp", "mp"), P("dp", "mp"), P(("dp", "mp"))),
        check_vma=False,
    )
```

```python
import functools

import jax
import jax.numpy as jnp
from jax import lax
from jax.experimental import pallas as pl
from jax.experimental.pallas import tpu as pltpu
from jax.sharding import PartitionSpec as P

MESH = pl.DeviceIdType.MESH
F32 = jnp.float32
BF16 = jnp.bfloat16
EPSILON = 1e-06
LOG2E = 1.4426950408889634
TURN = 16
TILE_ROWS = 512
CHUNK = 256
SMALL_PARTS = 4
STORES = 4


def kernel(
    image,
    text,
    sharpness,
    offset,
    image_out,
    text_out,
    loss_out,
    image_raw,
    text_raw,
    image_unit,
    image_rows,
    text_unit,
    image_acc,
    text_acc,
    far_send,
    far_recv,
    dots,
    far_dots,
    row_dots,
    products,
    logs,
    image_inverse,
    text_inverse,
    image_ss,
    image_rs,
    text_ss,
    text_rs,
    whole_ss,
    whole_rs,
    pass_ss,
    pass_rs,
    far_ss,
    far_rs,
    dot_ss,
    dot_rs,
    local_sem,
    out_sem,
    go_sem,
):
    half, rows = image.shape
    chunks = rows // CHUNK
    halves = rows // TILE_ROWS
    blocks = lax.axis_size("dp")
    dp = lax.axis_index("dp")
    mp = lax.axis_index("mp")
    core = lax.rem(dp, 2)
    turn_next = (lax.rem(dp, TURN) == TURN - 1).astype(jnp.int32)
    turn_prev = (lax.rem(dp, TURN) == 0).astype(jnp.int32)
    partner = (dp, 1 - mp)
    following = (lax.rem(dp + 1, blocks), mp + turn_next * (1 - 2 * mp))
    preceding = (lax.rem(dp + blocks - 1, blocks), mp + turn_prev * (1 - 2 * mp))
    own_slot = 1 - core
    prev_slot = core
    prev_offset = pl.multiple_of(turn_prev * half, half)

    def span(start, size):
        return pl.ds(pl.multiple_of(start, size), size)

    def columns(j):
        return span(j * CHUNK, CHUNK)

    def remote(src, dst, send, recv, device):
        return pltpu.make_async_remote_copy(
            src_ref=src,
            dst_ref=dst,
            send_sem=send,
            recv_sem=recv,
            device_id=device,
            device_id_type=MESH,
        )

    def image_copy(j):
        return remote(
            image.at[:, columns(j)],
            image_raw.at[pl.ds(half, half), columns(j)],
            image_ss.at[j],
            image_rs.at[j],
            partner,
        )

    def text_copy(j):
        return remote(
            text.at[:, columns(j)],
            text_raw.at[own_slot, pl.ds(half, half), columns(j)],
            text_ss.at[j],
            text_rs.at[j],
            partner,
        )

    def whole_copy(slot, turned):
        return remote(
            text,
            text_raw.at[slot, span(turned * half, half), :],
            whole_ss.at[0],
            whole_rs.at[0],
            following,
        )

    def pass_copy(slot, turned, j):
        return remote(
            text_raw.at[own_slot, pl.ds(half, half), columns(j)],
            text_raw.at[slot, span((1 - turned) * half, half), columns(j)],
            pass_ss.at[j],
            pass_rs.at[j],
            following,
        )

    def far_copy(j):
        return remote(
            far_send.at[:, columns(j)],
            far_recv.at[:, columns(j)],
            far_ss.at[j],
            far_rs.at[j],
            preceding,
        )

    def dot_copy(j):
        return remote(
            dots.at[prev_slot, :, columns(j)],
            far_dots.at[:, columns(j)],
            dot_ss.at[j],
            dot_rs.at[j],
            preceding,
        )

    def image_here():
        return pltpu.make_async_copy(image, image_raw.at[pl.ds(0, half), :], local_sem.at[0])

    def text_here():
        return pltpu.make_async_copy(
            text, text_raw.at[own_slot, pl.ds(0, half), :], local_sem.at[1]
        )

    def image_result(j):
        return pltpu.make_async_copy(
            image_acc.at[:, columns(j)], image_out.at[:, columns(j)], out_sem.at[0, j]
        )

    def text_result(j):
        return pltpu.make_async_copy(
            text_acc.at[own_slot, :, columns(j)], text_out.at[:, columns(j)], out_sem.at[1, j]
        )

    def each(count, body):
        def step(j, carry):
            body(j)
            return carry

        lax.fori_loop(0, count, step, 0)

    scale = sharpness[0]
    slope = scale * LOG2E
    shift = offset[0] * LOG2E

    def normal(raw):
        values = raw.astype(F32)
        inverse = lax.rsqrt(jnp.sum(values * values, axis=0, keepdims=True) + EPSILON)
        return (values * inverse).astype(BF16), inverse

    def prepare_text(slot, j):
        unit, inverse = normal(text_raw[slot, :, columns(j)])
        text_unit[slot, :, columns(j)] = unit
        text_inverse[slot, 0:1, columns(j)] = inverse

    def prepare_image(j):
        unit, inverse = normal(image_raw[:, columns(j)])
        image_unit[:, columns(j)] = unit
        image_inverse[0:1, columns(j)] = inverse
        image_rows[columns(j), :] = unit.T

    def tile(slot, own, row, height, column, width, place, parts=1):
        there = pl.ds(pl.multiple_of(column, CHUNK), width)
        size = height // parts
        spans = [pl.ds(pl.multiple_of(row + i * size, size), size) for i in range(parts)]
        scores = [
            jnp.dot(image_rows[here, :], text_unit[slot, :, there], preferred_element_type=F32)
            for here in spans
        ]
        grads = []
        inner = jnp.zeros((1, width), F32)
        for i, (here, dot) in enumerate(zip(spans, scores)):
            power = dot * slope + shift
            if own:
                first = lax.broadcasted_iota(jnp.int32, dot.shape, 0) + (row + i * size - column)
                paired = first == lax.broadcasted_iota(jnp.int32, dot.shape, 1)
                power = jnp.where(paired, -power, power)
            term = jnp.exp2(power)
            total = term + 1.0
            weight = (term * scale) / total
            if own:
                weight = jnp.where(paired, -weight, weight)
            product = weight * dot
            summed, multiplied = product[:, :128], total[:, :128]
            for lane in range(128, width, 128):
                summed += product[:, lane : lane + 128]
                multiplied *= total[:, lane : lane + 128]
            row_dots[here, :] += summed
            products[here, :] *= multiplied
            inner += jnp.sum(product, axis=0, keepdims=True)
            rounded = weight.astype(BF16)
            image_acc[:, here] += lax.dot_general(
                text_unit[slot, pl.ds(0, half), there],
                rounded,
                (((1,), (1,)), ((), ())),
                preferred_element_type=F32,
            )
            grads.append(
                jnp.dot(image_unit[pl.ds(place, half), here], rounded, preferred_element_type=F32)
            )
        dots[slot, 0:1, there] += inner
        text_acc[slot, :, there] += sum(grads[1:], grads[0])

    def take_logs():
        logs[...] += jnp.log(products[...])
        products[...] = jnp.ones_like(products)

    def send_far(slot, j):
        far_send[:, columns(j)] = text_acc[slot, :, columns(j)].astype(BF16)
        far_copy(j).start()
        dot_copy(j).start()

    def finish_image():
        image_dot = jnp.sum(row_dots[...].T, axis=0, keepdims=True)
        for j in range(chunks):
            cut = slice(j * CHUNK, (j + 1) * CHUNK)
            back = image_unit[0:half, cut].astype(F32)
            image_acc[:, cut] = (image_acc[:, cut] - back * image_dot[:, cut]) * image_inverse[
                0:1, cut
            ]
            image_result(j).start()

    def finish_loss():
        take_logs()
        image_inverse[0:1, :] = jnp.sum(logs[...].T, axis=0, keepdims=True) / (2 * rows)
        share = rows // 2
        loss_out[...] = image_inverse[0:1, span(mp * share, share)]

    def finish_text(slot, j):
        cut = columns(j)
        far_copy(j).wait_recv()
        dot_copy(j).wait_recv()
        total = text_acc[slot, :, cut] + far_recv[:, cut].astype(F32)
        dot = dots[slot, 0:1, cut] + far_dots[0:1, cut]
        back = text_unit[slot, pl.ds(0, half), cut].astype(F32)
        text_acc[slot, :, cut] = (total - back * dot) * text_inverse[slot, 0:1, cut]
        text_result(j).start()

    image_here().start()
    text_here().start()
    barrier = pltpu.get_barrier_semaphore()
    for device in (partner, following, preceding):
        pl.semaphore_signal(barrier, inc=1, device_id=device, device_id_type=MESH)
    pl.semaphore_wait(barrier, 3)

    @pl.when(core == 0)
    def _():
        each(chunks, lambda j: image_copy(j).start())

    @pl.when(core == 1)
    def _():
        each(chunks, lambda j: text_copy(j).start())
        each(chunks, lambda j: image_copy(j).start())

    whole_copy(own_slot, turn_next).start()

    image_acc[...] = jnp.zeros_like(image_acc)
    text_acc[...] = jnp.zeros_like(text_acc)
    dots[...] = jnp.zeros_like(dots)
    row_dots[...] = jnp.zeros_like(row_dots)
    logs[...] = jnp.zeros_like(logs)
    products[...] = jnp.ones_like(products)
    image_here().wait()
    text_here().wait()

    @pl.when(core == 0)
    def _():
        def arrive(j):
            image_copy(j).wait_recv()
            prepare_image(j)

        each(chunks, arrive)
        whole_copy(prev_slot, turn_prev).wait_recv()

        def first(i):
            def ready(j):
                pass_copy(prev_slot, turn_prev, 2 * i + j).wait_recv()
                prepare_text(0, 2 * i + j)

            each(2, ready)
            tile(0, False, 0, rows, 2 * i * CHUNK, 2 * CHUNK, prev_offset)
            each(2, lambda j: send_far(0, 2 * i + j))

        each(chunks // 2, first)
        pl.semaphore_wait(go_sem, 1)
        each(chunks, lambda j: text_copy(j).start())
        take_logs()

        def ready(j):
            text_copy(j).wait_recv()
            pass_copy(own_slot, turn_next, j).start()
            prepare_text(1, j)

        each(2, ready)
        tile(1, True, 0, rows, 0, 2 * CHUNK, 0)

        def second(j):
            ready(j + 2)
            tile(1, True, 0, rows, (j + 2) * CHUNK, CHUNK, 0, SMALL_PARTS)
            finish_text(1, j)

        each(chunks - 2, second)
        finish_image()
        finish_loss()
        each(2, lambda j: finish_text(1, chunks - 2 + j))

    @pl.when(core == 1)
    def _():
        def ready(j):
            text_copy(j).wait_recv()
            pass_copy(own_slot, turn_next, j).start()
            prepare_text(0, j)

        each(chunks, ready)

        per_half = TILE_ROWS // CHUNK

        def first(h):
            image_copy(h * per_half).wait_recv()
            image_copy(h * per_half).wait_send()

            @pl.when(h == halves - 1)
            def _():
                pl.semaphore_signal(go_sem, inc=1, device_id=preceding, device_id_type=MESH)

            prepare_image(h * per_half)

            def arrive(i):
                image_copy(h * per_half + i + 1).wait_recv()
                prepare_image(h * per_half + i + 1)

            each(per_half - 1, arrive)
            each(
                2,
                lambda i: tile(0, True, h * TILE_ROWS, TILE_ROWS, 2 * i * CHUNK, 2 * CHUNK, 0),
            )

        each(halves, first)
        take_logs()
        whole_copy(prev_slot, turn_prev).wait_recv()

        def come(j):
            pass_copy(prev_slot, turn_prev, j).wait_recv()
            prepare_text(1, j)

        each(2, come)
        tile(1, False, 0, rows, 0, 2 * CHUNK, 0)
        each(2, lambda j: send_far(1, j))

        def second(j):
            come(j + 2)
            tile(1, False, 0, rows, (j + 2) * CHUNK, CHUNK, 0, SMALL_PARTS)
            send_far(1, j + 2)
            each(2, lambda i: finish_text(0, 2 * j + i))

        each(chunks - 2, second)
        finish_image()
        finish_loss()

    def settle(j):
        text_copy(j).wait_send()
        pass_copy(own_slot, turn_next, j).wait_send()
        far_copy(j).wait_send()
        dot_copy(j).wait_send()
        image_result(j).wait()
        text_result(j).wait()

    each(chunks, settle)
    whole_copy(own_slot, turn_next).wait_send()

    @pl.when(core == 0)
    def _():
        each(chunks, lambda j: image_copy(j).wait_send())

    @pl.when(core == 1)
    def _():
        per_half = TILE_ROWS // CHUNK

        def rest(j):
            @pl.when(lax.rem(j, per_half) != 0)
            def _():
                image_copy(j).wait_send()

        each(chunks, rest)


def store(image_in, text_in, loss_in, image_out, text_out, loss_out, sem):
    size = image_in.shape[0] // STORES
    loss_out[...] = loss_in[...]
    copies = []
    for i in range(STORES):
        part = pl.ds(i * size, size)
        copies.append(pltpu.make_async_copy(image_in.at[part, :], image_out.at[part, :], sem.at[2 * i]))
        copies.append(
            pltpu.make_async_copy(text_in.at[part, :], text_out.at[part, :], sem.at[2 * i + 1])
        )
    for copy in copies:
        copy.start()
    for copy in copies:
        copy.wait()


def per_device(picture_vectors, caption_vectors, sharpness_coefficient, affinity_offset):
    rows, half = picture_vectors.shape
    chunks = rows // CHUNK
    width = 2 * half
    anywhere = pl.BlockSpec(memory_space=pl.ANY)
    held = pl.BlockSpec(memory_space=pltpu.HBM)
    inside = pl.BlockSpec(memory_space=pltpu.VMEM)
    scalar = pl.BlockSpec(memory_space=pltpu.SMEM)
    dma = pltpu.SemaphoreType.DMA
    image_grad, text_grad, row_loss = pl.pallas_call(
        kernel,
        out_shape=(
            jax.ShapeDtypeStruct((half, rows), F32),
            jax.ShapeDtypeStruct((half, rows), F32),
            jax.ShapeDtypeStruct((1, rows // 2), F32),
        ),
        in_specs=[held, held, scalar, scalar],
        out_specs=(anywhere, anywhere, pl.BlockSpec(memory_space=pltpu.VMEM)),
        scratch_shapes=[
            pltpu.VMEM((width, rows), BF16),
            pltpu.VMEM((2, width, rows), BF16),
            pltpu.VMEM((width, rows), BF16),
            pltpu.VMEM((rows, width), BF16),
            pltpu.VMEM((2, width, rows), BF16),
            pltpu.VMEM((half, rows), F32),
            pltpu.VMEM((2, half, rows), F32),
            pltpu.VMEM((half, rows), BF16),
            pltpu.VMEM((half, rows), BF16),
            pltpu.VMEM((2, 8, rows), F32),
            pltpu.VMEM((8, rows), F32),
            pltpu.VMEM((rows, 128), F32),
            pltpu.VMEM((rows, 128), F32),
            pltpu.VMEM((rows, 128), F32),
            pltpu.VMEM((8, rows), F32),
            pltpu.VMEM((2, 8, rows), F32),
            dma((chunks,)),
            dma((chunks,)),
            dma((chunks,)),
            dma((chunks,)),
            dma((1,)),
            dma((1,)),
            dma((chunks,)),
            dma((chunks,)),
            dma((chunks,)),
            dma((chunks,)),
            dma((chunks,)),
            dma((chunks,)),
            dma((2,)),
            dma((2, chunks)),
            pltpu.SemaphoreType.REGULAR,
        ],
        compiler_params=pltpu.CompilerParams(
            collective_id=0, has_side_effects=True, vmem_limit_bytes=44 * 1024 * 1024
        ),
        cost_estimate=pl.CostEstimate(
            flops=8 * rows * rows * width, bytes_accessed=12 * half * rows, transcendentals=0
        ),
    )(
        pltpu.with_memory_space_constraint(picture_vectors.T, pltpu.HBM),
        pltpu.with_memory_space_constraint(caption_vectors.T, pltpu.HBM),
        sharpness_coefficient,
        affinity_offset,
    )
    image_grad, text_grad, row_loss = pl.pallas_call(
        store,
        out_shape=(
            jax.ShapeDtypeStruct((half, rows), F32),
            jax.ShapeDtypeStruct((half, rows), F32),
            jax.ShapeDtypeStruct((1, rows // 2), F32),
        ),
        in_specs=[anywhere, anywhere, inside],
        out_specs=(anywhere, anywhere, inside),
        scratch_shapes=[dma((2 * STORES,))],
        compiler_params=pltpu.CompilerParams(vmem_limit_bytes=1024 * 1024),
    )(image_grad, text_grad, row_loss)
    return image_grad.T, text_grad.T, row_loss.reshape(rows // 2)


def solution(mesh):
    placed = (P("dp", "mp"), P("dp", "mp"), P(), P())
    return jax.shard_map(
        per_device,
        mesh=mesh,
        in_specs=placed,
        out_specs=(P("dp", "mp"), P("dp", "mp"), P(("dp", "mp"))),
        check_vma=False,
    )
```

```python
import functools

import jax
import jax.numpy as jnp
from jax import lax
from jax.experimental import pallas as pl
from jax.experimental.pallas import tpu as pltpu
from jax.sharding import PartitionSpec as P

MESH = pl.DeviceIdType.MESH
F32 = jnp.float32
BF16 = jnp.bfloat16
EPSILON = 1e-06
LOG2E = 1.4426950408889634
TURN = 16
TILE_ROWS = 512
CHUNK = 256
SMALL_PARTS = 4
STORES = 4


def kernel(
    image,
    text,
    sharpness,
    offset,
    image_out,
    text_out,
    loss_out,
    image_raw,
    text_raw,
    image_unit,
    image_rows,
    text_unit,
    image_acc,
    text_acc,
    far_send,
    far_recv,
    dots,
    far_dots,
    row_dots,
    products,
    logs,
    image_inverse,
    text_inverse,
    image_ss,
    image_rs,
    text_ss,
    text_rs,
    whole_ss,
    whole_rs,
    pass_ss,
    pass_rs,
    far_ss,
    far_rs,
    dot_ss,
    dot_rs,
    local_sem,
    out_sem,
    go_sem,
):
    half, rows = image.shape
    chunks = rows // CHUNK
    halves = rows // TILE_ROWS
    blocks = lax.axis_size("dp")
    dp = lax.axis_index("dp")
    mp = lax.axis_index("mp")
    core = lax.rem(dp, 2)
    turn_next = (lax.rem(dp, TURN) == TURN - 1).astype(jnp.int32)
    turn_prev = (lax.rem(dp, TURN) == 0).astype(jnp.int32)
    partner = (dp, 1 - mp)
    following = (lax.rem(dp + 1, blocks), mp + turn_next * (1 - 2 * mp))
    preceding = (lax.rem(dp + blocks - 1, blocks), mp + turn_prev * (1 - 2 * mp))
    own_slot = 1 - core
    prev_slot = core
    prev_offset = pl.multiple_of(turn_prev * half, half)

    def span(start, size):
        return pl.ds(pl.multiple_of(start, size), size)

    def columns(j):
        return span(j * CHUNK, CHUNK)

    def remote(src, dst, send, recv, device):
        return pltpu.make_async_remote_copy(
            src_ref=src,
            dst_ref=dst,
            send_sem=send,
            recv_sem=recv,
            device_id=device,
            device_id_type=MESH,
        )

    def image_copy(j):
        return remote(
            image.at[:, columns(j)],
            image_raw.at[pl.ds(half, half), columns(j)],
            image_ss.at[j],
            image_rs.at[j],
            partner,
        )

    def text_copy(j):
        return remote(
            text.at[:, columns(j)],
            text_raw.at[own_slot, pl.ds(half, half), columns(j)],
            text_ss.at[j],
            text_rs.at[j],
            partner,
        )

    def whole_copy(slot, turned):
        return remote(
            text,
            text_raw.at[slot, span(turned * half, half), :],
            whole_ss.at[0],
            whole_rs.at[0],
            following,
        )

    def pass_copy(slot, turned, j):
        return remote(
            text_raw.at[own_slot, pl.ds(half, half), columns(j)],
            text_raw.at[slot, span((1 - turned) * half, half), columns(j)],
            pass_ss.at[j],
            pass_rs.at[j],
            following,
        )

    def far_copy(j):
        return remote(
            far_send.at[:, columns(j)],
            far_recv.at[:, columns(j)],
            far_ss.at[j],
            far_rs.at[j],
            preceding,
        )

    def dot_copy(j):
        return remote(
            dots.at[prev_slot, :, columns(j)],
            far_dots.at[:, columns(j)],
            dot_ss.at[j],
            dot_rs.at[j],
            preceding,
        )

    def image_here():
        return pltpu.make_async_copy(image, image_raw.at[pl.ds(0, half), :], local_sem.at[0])

    def text_here():
        return pltpu.make_async_copy(
            text, text_raw.at[own_slot, pl.ds(0, half), :], local_sem.at[1]
        )

    def image_result(j):
        return pltpu.make_async_copy(
            image_acc.at[:, columns(j)], image_out.at[:, columns(j)], out_sem.at[0, j]
        )

    def text_result(j):
        return pltpu.make_async_copy(
            text_acc.at[own_slot, :, columns(j)], text_out.at[:, columns(j)], out_sem.at[1, j]
        )

    def each(count, body):
        def step(j, carry):
            body(j)
            return carry

        lax.fori_loop(0, count, step, 0)

    scale = sharpness[0]
    slope = scale * LOG2E
    shift = offset[0] * LOG2E

    def normal(raw):
        values = raw.astype(F32)
        inverse = lax.rsqrt(jnp.sum(values * values, axis=0, keepdims=True) + EPSILON)
        return (values * inverse).astype(BF16), inverse

    def prepare_text(slot, j):
        unit, inverse = normal(text_raw[slot, :, columns(j)])
        text_unit[slot, :, columns(j)] = unit
        text_inverse[slot, 0:1, columns(j)] = inverse

    def prepare_image(j):
        unit, inverse = normal(image_raw[:, columns(j)])
        image_unit[:, columns(j)] = unit
        image_inverse[0:1, columns(j)] = inverse
        image_rows[columns(j), :] = unit.T

    def tile(slot, own, row, height, column, width, place, parts=1):
        there = pl.ds(pl.multiple_of(column, CHUNK), width)
        size = height // parts
        spans = [pl.ds(pl.multiple_of(row + i * size, size), size) for i in range(parts)]
        scores = [
            jnp.dot(image_rows[here, :], text_unit[slot, :, there], preferred_element_type=F32)
            for here in spans
        ]
        grads = []
        inner = jnp.zeros((1, width), F32)
        for i, (here, dot) in enumerate(zip(spans, scores)):
            power = dot * slope + shift
            if own:
                first = lax.broadcasted_iota(jnp.int32, dot.shape, 0) + (row + i * size - column)
                paired = first == lax.broadcasted_iota(jnp.int32, dot.shape, 1)
                power = jnp.where(paired, -power, power)
            term = jnp.exp2(power)
            total = term + 1.0
            weight = (term * scale) / total
            if own:
                weight = jnp.where(paired, -weight, weight)
            product = weight * dot
            summed, multiplied = product[:, :128], total[:, :128]
            for lane in range(128, width, 128):
                summed += product[:, lane : lane + 128]
                multiplied *= total[:, lane : lane + 128]
            row_dots[here, :] += summed
            products[here, :] *= multiplied
            inner += jnp.sum(product, axis=0, keepdims=True)
            rounded = weight.astype(BF16)
            image_acc[:, here] += lax.dot_general(
                text_unit[slot, pl.ds(0, half), there],
                rounded,
                (((1,), (1,)), ((), ())),
                preferred_element_type=F32,
            )
            grads.append(
                jnp.dot(image_unit[pl.ds(place, half), here], rounded, preferred_element_type=F32)
            )
        dots[slot, 0:1, there] += inner
        text_acc[slot, :, there] += sum(grads[1:], grads[0])

    def take_logs():
        logs[...] += jnp.log(products[...])
        products[...] = jnp.ones_like(products)

    def send_far(slot, j):
        far_send[:, columns(j)] = text_acc[slot, :, columns(j)].astype(BF16)
        far_copy(j).start()
        dot_copy(j).start()

    def finish_image():
        image_dot = jnp.sum(row_dots[...].T, axis=0, keepdims=True)
        for j in range(chunks):
            cut = slice(j * CHUNK, (j + 1) * CHUNK)
            back = image_unit[0:half, cut].astype(F32)
            image_acc[:, cut] = (image_acc[:, cut] - back * image_dot[:, cut]) * image_inverse[
                0:1, cut
            ]
            image_result(j).start()

    def finish_loss():
        take_logs()
        image_inverse[0:1, :] = jnp.sum(logs[...].T, axis=0, keepdims=True) / (2 * rows)
        share = rows // 2
        loss_out[...] = image_inverse[0:1, span(mp * share, share)]

    def finish_text(slot, j):
        cut = columns(j)
        far_copy(j).wait_recv()
        dot_copy(j).wait_recv()
        total = text_acc[slot, :, cut] + far_recv[:, cut].astype(F32)
        dot = dots[slot, 0:1, cut] + far_dots[0:1, cut]
        back = text_unit[slot, pl.ds(0, half), cut].astype(F32)
        text_acc[slot, :, cut] = (total - back * dot) * text_inverse[slot, 0:1, cut]
        text_result(j).start()

    image_here().start()
    text_here().start()
    barrier = pltpu.get_barrier_semaphore()
    for device in (partner, preceding):
        pl.semaphore_signal(barrier, inc=1, device_id=device, device_id_type=MESH)
    pl.semaphore_wait(barrier, 2)

    @pl.when(core == 0)
    def _():
        each(chunks, lambda j: image_copy(j).start())

    @pl.when(core == 1)
    def _():
        each(chunks, lambda j: text_copy(j).start())
        each(chunks, lambda j: image_copy(j).start())

    whole_copy(own_slot, turn_next).start()

    image_acc[...] = jnp.zeros_like(image_acc)
    text_acc[...] = jnp.zeros_like(text_acc)
    dots[...] = jnp.zeros_like(dots)
    row_dots[...] = jnp.zeros_like(row_dots)
    logs[...] = jnp.zeros_like(logs)
    products[...] = jnp.ones_like(products)
    image_here().wait()
    text_here().wait()

    @pl.when(core == 0)
    def _():
        def arrive(j):
            image_copy(j).wait_recv()
            prepare_image(j)

        each(chunks, arrive)
        whole_copy(prev_slot, turn_prev).wait_recv()

        def first(i):
            def ready(j):
                pass_copy(prev_slot, turn_prev, 2 * i + j).wait_recv()
                prepare_text(0, 2 * i + j)

            @pl.when(i == 1)
            def _():
                pl.semaphore_wait(go_sem, 1)
                each(chunks, lambda j: text_copy(j).start())

            each(2, ready)
            tile(0, False, 0, rows, 2 * i * CHUNK, 2 * CHUNK, prev_offset)
            each(2, lambda j: send_far(0, 2 * i + j))

        each(chunks // 2, first)
        take_logs()

        def ready(j):
            text_copy(j).wait_recv()
            pass_copy(own_slot, turn_next, j).start()
            prepare_text(1, j)

        each(2, ready)
        tile(1, True, 0, rows, 0, 2 * CHUNK, 0)

        def second(j):
            ready(j + 2)
            tile(1, True, 0, rows, (j + 2) * CHUNK, CHUNK, 0, SMALL_PARTS)
            finish_text(1, j)

        each(chunks - 2, second)
        finish_image()
        finish_loss()
        each(2, lambda j: finish_text(1, chunks - 2 + j))

    @pl.when(core == 1)
    def _():
        def ready(j):
            text_copy(j).wait_recv()
            pass_copy(own_slot, turn_next, j).start()
            prepare_text(0, j)

        each(chunks, ready)
        whole_copy(prev_slot, turn_prev).wait_recv()

        per_half = TILE_ROWS // CHUNK

        def first(h):
            image_copy(h * per_half).wait_recv()
            image_copy(h * per_half).wait_send()

            @pl.when(h == halves - 1)
            def _():
                pl.semaphore_signal(go_sem, inc=1, device_id=preceding, device_id_type=MESH)

            prepare_image(h * per_half)

            def arrive(i):
                image_copy(h * per_half + i + 1).wait_recv()
                prepare_image(h * per_half + i + 1)

            each(per_half - 1, arrive)
            each(
                2,
                lambda i: tile(0, True, h * TILE_ROWS, TILE_ROWS, 2 * i * CHUNK, 2 * CHUNK, 0),
            )

        each(halves, first)
        take_logs()

        def come(j):
            pass_copy(prev_slot, turn_prev, j).wait_recv()
            prepare_text(1, j)

        each(2, come)
        tile(1, False, 0, rows, 0, 2 * CHUNK, 0)
        each(2, lambda j: send_far(1, j))

        def second(j):
            come(j + 2)
            tile(1, False, 0, rows, (j + 2) * CHUNK, CHUNK, 0, SMALL_PARTS)
            send_far(1, j + 2)
            each(2, lambda i: finish_text(0, 2 * j + i))

        each(chunks - 2, second)
        finish_image()
        finish_loss()

    def settle(j):
        text_copy(j).wait_send()
        pass_copy(own_slot, turn_next, j).wait_send()
        far_copy(j).wait_send()
        dot_copy(j).wait_send()
        image_result(j).wait()
        text_result(j).wait()

    each(chunks, settle)
    whole_copy(own_slot, turn_next).wait_send()

    @pl.when(core == 0)
    def _():
        each(chunks, lambda j: image_copy(j).wait_send())

    @pl.when(core == 1)
    def _():
        per_half = TILE_ROWS // CHUNK

        def rest(j):
            @pl.when(lax.rem(j, per_half) != 0)
            def _():
                image_copy(j).wait_send()

        each(chunks, rest)


def store(image_in, text_in, loss_in, image_out, text_out, loss_out, sem):
    size = image_in.shape[0] // STORES
    loss_out[...] = loss_in[...]
    copies = []
    for i in range(STORES):
        part = pl.ds(i * size, size)
        copies.append(pltpu.make_async_copy(image_in.at[part, :], image_out.at[part, :], sem.at[2 * i]))
        copies.append(
            pltpu.make_async_copy(text_in.at[part, :], text_out.at[part, :], sem.at[2 * i + 1])
        )
    for copy in copies:
        copy.start()
    for copy in copies:
        copy.wait()


def per_device(picture_vectors, caption_vectors, sharpness_coefficient, affinity_offset):
    rows, half = picture_vectors.shape
    chunks = rows // CHUNK
    width = 2 * half
    anywhere = pl.BlockSpec(memory_space=pl.ANY)
    held = pl.BlockSpec(memory_space=pltpu.HBM)
    inside = pl.BlockSpec(memory_space=pltpu.VMEM)
    scalar = pl.BlockSpec(memory_space=pltpu.SMEM)
    dma = pltpu.SemaphoreType.DMA
    image_grad, text_grad, row_loss = pl.pallas_call(
        kernel,
        out_shape=(
            jax.ShapeDtypeStruct((half, rows), F32),
            jax.ShapeDtypeStruct((half, rows), F32),
            jax.ShapeDtypeStruct((1, rows // 2), F32),
        ),
        in_specs=[held, held, scalar, scalar],
        out_specs=(anywhere, anywhere, pl.BlockSpec(memory_space=pltpu.VMEM)),
        scratch_shapes=[
            pltpu.VMEM((width, rows), BF16),
            pltpu.VMEM((2, width, rows), BF16),
            pltpu.VMEM((width, rows), BF16),
            pltpu.VMEM((rows, width), BF16),
            pltpu.VMEM((2, width, rows), BF16),
            pltpu.VMEM((half, rows), F32),
            pltpu.VMEM((2, half, rows), F32),
            pltpu.VMEM((half, rows), BF16),
            pltpu.VMEM((half, rows), BF16),
            pltpu.VMEM((2, 8, rows), F32),
            pltpu.VMEM((8, rows), F32),
            pltpu.VMEM((rows, 128), F32),
            pltpu.VMEM((rows, 128), F32),
            pltpu.VMEM((rows, 128), F32),
            pltpu.VMEM((8, rows), F32),
            pltpu.VMEM((2, 8, rows), F32),
            dma((chunks,)),
            dma((chunks,)),
            dma((chunks,)),
            dma((chunks,)),
            dma((1,)),
            dma((1,)),
            dma((chunks,)),
            dma((chunks,)),
            dma((chunks,)),
            dma((chunks,)),
            dma((chunks,)),
            dma((chunks,)),
            dma((2,)),
            dma((2, chunks)),
            pltpu.SemaphoreType.REGULAR,
        ],
        compiler_params=pltpu.CompilerParams(
            collective_id=0, has_side_effects=True, vmem_limit_bytes=44 * 1024 * 1024
        ),
        cost_estimate=pl.CostEstimate(
            flops=8 * rows * rows * width, bytes_accessed=12 * half * rows, transcendentals=0
        ),
    )(
        pltpu.with_memory_space_constraint(picture_vectors.T, pltpu.HBM),
        pltpu.with_memory_space_constraint(caption_vectors.T, pltpu.HBM),
        sharpness_coefficient,
        affinity_offset,
    )
    image_grad, text_grad, row_loss = pl.pallas_call(
        store,
        out_shape=(
            jax.ShapeDtypeStruct((half, rows), F32),
            jax.ShapeDtypeStruct((half, rows), F32),
            jax.ShapeDtypeStruct((1, rows // 2), F32),
        ),
        in_specs=[anywhere, anywhere, inside],
        out_specs=(anywhere, anywhere, inside),
        scratch_shapes=[dma((2 * STORES,))],
        compiler_params=pltpu.CompilerParams(vmem_limit_bytes=1024 * 1024),
    )(image_grad, text_grad, row_loss)
    return image_grad.T, text_grad.T, row_loss.reshape(rows // 2)


def solution(mesh):
    placed = (P("dp", "mp"), P("dp", "mp"), P(), P())
    return jax.shard_map(
        per_device,
        mesh=mesh,
        in_specs=placed,
        out_specs=(P("dp", "mp"), P("dp", "mp"), P(("dp", "mp"))),
        check_vma=False,
    )
```

```python
import functools

import jax
import jax.numpy as jnp
from jax import lax
from jax.experimental import pallas as pl
from jax.experimental.pallas import tpu as pltpu
from jax.sharding import PartitionSpec as P

MESH = pl.DeviceIdType.MESH
F32 = jnp.float32
BF16 = jnp.bfloat16
EPSILON = 1e-06
LOG2E = 1.4426950408889634
TURN = 16
TILE_ROWS = 512
CHUNK = 256
SMALL_PARTS = 4
STORES = 4


def kernel(
    image,
    text,
    sharpness,
    offset,
    image_out,
    text_out,
    loss_out,
    image_raw,
    text_raw,
    image_unit,
    image_rows,
    text_unit,
    image_acc,
    text_acc,
    far_send,
    far_recv,
    dots,
    far_dots,
    row_dots,
    products,
    logs,
    image_inverse,
    text_inverse,
    image_ss,
    image_rs,
    text_ss,
    text_rs,
    whole_ss,
    whole_rs,
    pass_ss,
    pass_rs,
    far_ss,
    far_rs,
    dot_ss,
    dot_rs,
    local_sem,
    go_sem,
):
    half, rows = image.shape
    chunks = rows // CHUNK
    halves = rows // TILE_ROWS
    blocks = lax.axis_size("dp")
    dp = lax.axis_index("dp")
    mp = lax.axis_index("mp")
    core = lax.rem(dp, 2)
    turn_next = (lax.rem(dp, TURN) == TURN - 1).astype(jnp.int32)
    turn_prev = (lax.rem(dp, TURN) == 0).astype(jnp.int32)
    partner = (dp, 1 - mp)
    following = (lax.rem(dp + 1, blocks), mp + turn_next * (1 - 2 * mp))
    preceding = (lax.rem(dp + blocks - 1, blocks), mp + turn_prev * (1 - 2 * mp))
    own_slot = 1 - core
    prev_slot = core
    prev_offset = pl.multiple_of(turn_prev * half, half)

    def span(start, size):
        return pl.ds(pl.multiple_of(start, size), size)

    def columns(j):
        return span(j * CHUNK, CHUNK)

    def remote(src, dst, send, recv, device):
        return pltpu.make_async_remote_copy(
            src_ref=src,
            dst_ref=dst,
            send_sem=send,
            recv_sem=recv,
            device_id=device,
            device_id_type=MESH,
        )

    def image_copy(j):
        return remote(
            image.at[:, columns(j)],
            image_raw.at[pl.ds(half, half), columns(j)],
            image_ss.at[j],
            image_rs.at[j],
            partner,
        )

    def text_copy(j):
        return remote(
            text.at[:, columns(j)],
            text_raw.at[own_slot, pl.ds(half, half), columns(j)],
            text_ss.at[j],
            text_rs.at[j],
            partner,
        )

    def whole_copy(slot, turned):
        return remote(
            text,
            text_raw.at[slot, span(turned * half, half), :],
            whole_ss.at[0],
            whole_rs.at[0],
            following,
        )

    def pass_copy(slot, turned, j):
        return remote(
            text_raw.at[own_slot, pl.ds(half, half), columns(j)],
            text_raw.at[slot, span((1 - turned) * half, half), columns(j)],
            pass_ss.at[j],
            pass_rs.at[j],
            following,
        )

    def far_copy(j):
        return remote(
            far_send.at[:, columns(j)],
            far_recv.at[:, columns(j)],
            far_ss.at[j],
            far_rs.at[j],
            preceding,
        )

    def dot_copy(j):
        return remote(
            dots.at[prev_slot, :, columns(j)],
            far_dots.at[:, columns(j)],
            dot_ss.at[j],
            dot_rs.at[j],
            preceding,
        )

    def image_here():
        return pltpu.make_async_copy(image, image_raw.at[pl.ds(0, half), :], local_sem.at[0])

    def text_here():
        return pltpu.make_async_copy(
            text, text_raw.at[own_slot, pl.ds(0, half), :], local_sem.at[1]
        )

    def each(count, body):
        def step(j, carry):
            body(j)
            return carry

        lax.fori_loop(0, count, step, 0)

    scale = sharpness[0]
    slope = scale * LOG2E
    shift = offset[0] * LOG2E

    def normal(raw):
        values = raw.astype(F32)
        inverse = lax.rsqrt(jnp.sum(values * values, axis=0, keepdims=True) + EPSILON)
        return (values * inverse).astype(BF16), inverse

    def prepare_text(slot, j):
        unit, inverse = normal(text_raw[slot, :, columns(j)])
        text_unit[slot, :, columns(j)] = unit
        text_inverse[slot, 0:1, columns(j)] = inverse

    def prepare_image(j):
        unit, inverse = normal(image_raw[:, columns(j)])
        image_unit[:, columns(j)] = unit
        image_inverse[0:1, columns(j)] = inverse
        image_rows[columns(j), :] = unit.T

    def tile(slot, own, row, height, column, width, place, parts=1):
        there = pl.ds(pl.multiple_of(column, CHUNK), width)
        size = height // parts
        spans = [pl.ds(pl.multiple_of(row + i * size, size), size) for i in range(parts)]
        scores = [
            jnp.dot(image_rows[here, :], text_unit[slot, :, there], preferred_element_type=F32)
            for here in spans
        ]
        grads = []
        inner = jnp.zeros((1, width), F32)
        for i, (here, dot) in enumerate(zip(spans, scores)):
            power = dot * slope + shift
            if own:
                first = lax.broadcasted_iota(jnp.int32, dot.shape, 0) + (row + i * size - column)
                paired = first == lax.broadcasted_iota(jnp.int32, dot.shape, 1)
                power = jnp.where(paired, -power, power)
            term = jnp.exp2(power)
            total = term + 1.0
            weight = (term * scale) / total
            if own:
                weight = jnp.where(paired, -weight, weight)
            product = weight * dot
            summed, multiplied = product[:, :128], total[:, :128]
            for lane in range(128, width, 128):
                summed += product[:, lane : lane + 128]
                multiplied *= total[:, lane : lane + 128]
            row_dots[here, :] += summed
            products[here, :] *= multiplied
            inner += jnp.sum(product, axis=0, keepdims=True)
            rounded = weight.astype(BF16)
            image_acc[:, here] += lax.dot_general(
                text_unit[slot, pl.ds(0, half), there],
                rounded,
                (((1,), (1,)), ((), ())),
                preferred_element_type=F32,
            )
            grads.append(
                jnp.dot(image_unit[pl.ds(place, half), here], rounded, preferred_element_type=F32)
            )
        dots[slot, 0:1, there] += inner
        text_acc[slot, :, there] += sum(grads[1:], grads[0])

    def take_logs():
        logs[...] += jnp.log(products[...])
        products[...] = jnp.ones_like(products)

    def send_far(slot, j):
        far_send[:, columns(j)] = text_acc[slot, :, columns(j)].astype(BF16)
        far_copy(j).start()
        dot_copy(j).start()

    def finish_image():
        image_dot = jnp.sum(row_dots[...].T, axis=0, keepdims=True)
        for j in range(chunks):
            cut = slice(j * CHUNK, (j + 1) * CHUNK)
            back = image_unit[0:half, cut].astype(F32)
            image_out[:, cut] = (image_acc[:, cut] - back * image_dot[:, cut]) * image_inverse[
                0:1, cut
            ]

    def finish_loss():
        take_logs()
        image_inverse[0:1, :] = jnp.sum(logs[...].T, axis=0, keepdims=True) / (2 * rows)
        share = rows // 2
        loss_out[...] = image_inverse[0:1, span(mp * share, share)]

    def finish_text(slot, j):
        cut = columns(j)
        far_copy(j).wait_recv()
        dot_copy(j).wait_recv()
        total = text_acc[slot, :, cut] + far_recv[:, cut].astype(F32)
        dot = dots[slot, 0:1, cut] + far_dots[0:1, cut]
        back = text_unit[slot, pl.ds(0, half), cut].astype(F32)
        text_out[:, cut] = (total - back * dot) * text_inverse[slot, 0:1, cut]

    barrier = pltpu.get_barrier_semaphore()
    for device in (partner, preceding):
        pl.semaphore_signal(barrier, inc=1, device_id=device, device_id_type=MESH)
    pl.semaphore_wait(barrier, 2)

    @pl.when(core == 0)
    def _():
        each(chunks, lambda j: image_copy(j).start())

    @pl.when(core == 1)
    def _():
        each(chunks, lambda j: text_copy(j).start())
        each(chunks, lambda j: image_copy(j).start())

    whole_copy(own_slot, turn_next).start()
    image_here().start()
    text_here().start()

    image_acc[...] = jnp.zeros_like(image_acc)
    text_acc[...] = jnp.zeros_like(text_acc)
    dots[...] = jnp.zeros_like(dots)
    row_dots[...] = jnp.zeros_like(row_dots)
    logs[...] = jnp.zeros_like(logs)
    products[...] = jnp.ones_like(products)
    image_here().wait()
    text_here().wait()

    @pl.when(core == 0)
    def _():
        def arrive(j):
            image_copy(j).wait_recv()
            prepare_image(j)

        each(chunks, arrive)
        whole_copy(prev_slot, turn_prev).wait_recv()

        def first(i):
            def ready(j):
                pass_copy(prev_slot, turn_prev, 2 * i + j).wait_recv()
                prepare_text(0, 2 * i + j)

            @pl.when(i == 1)
            def _():
                pl.semaphore_wait(go_sem, 1)
                each(chunks, lambda j: text_copy(j).start())

            each(2, ready)
            tile(0, False, 0, rows, 2 * i * CHUNK, 2 * CHUNK, prev_offset)
            each(2, lambda j: send_far(0, 2 * i + j))

        each(chunks // 2, first)
        take_logs()

        def ready(j):
            text_copy(j).wait_recv()
            pass_copy(own_slot, turn_next, j).start()
            prepare_text(1, j)

        each(2, ready)
        tile(1, True, 0, rows, 0, 2 * CHUNK, 0)

        def second(j):
            ready(j + 2)
            tile(1, True, 0, rows, (j + 2) * CHUNK, CHUNK, 0, SMALL_PARTS)
            finish_text(1, j)

        each(chunks - 2, second)
        finish_image()
        finish_loss()
        each(2, lambda j: finish_text(1, chunks - 2 + j))

    @pl.when(core == 1)
    def _():
        def ready(j):
            text_copy(j).wait_recv()
            pass_copy(own_slot, turn_next, j).start()
            prepare_text(0, j)

        each(chunks, ready)
        whole_copy(prev_slot, turn_prev).wait_recv()

        per_half = TILE_ROWS // CHUNK

        def first(h):
            image_copy(h * per_half).wait_recv()
            image_copy(h * per_half).wait_send()

            @pl.when(h == halves - 1)
            def _():
                pl.semaphore_signal(go_sem, inc=1, device_id=preceding, device_id_type=MESH)

            prepare_image(h * per_half)

            def arrive(i):
                image_copy(h * per_half + i + 1).wait_recv()
                prepare_image(h * per_half + i + 1)

            each(per_half - 1, arrive)
            each(
                2,
                lambda i: tile(0, True, h * TILE_ROWS, TILE_ROWS, 2 * i * CHUNK, 2 * CHUNK, 0),
            )

        each(halves, first)
        take_logs()

        def come(j):
            pass_copy(prev_slot, turn_prev, j).wait_recv()
            prepare_text(1, j)

        each(2, come)
        tile(1, False, 0, rows, 0, 2 * CHUNK, 0)
        each(2, lambda j: send_far(1, j))

        def second(j):
            each(2, lambda i: finish_text(0, 2 * j + i))
            come(j + 2)
            tile(1, False, 0, rows, (j + 2) * CHUNK, CHUNK, 0, SMALL_PARTS)
            send_far(1, j + 2)

        each(chunks - 2, second)
        finish_image()
        finish_loss()

    def settle(j):
        text_copy(j).wait_send()
        pass_copy(own_slot, turn_next, j).wait_send()
        far_copy(j).wait_send()
        dot_copy(j).wait_send()

    each(chunks, settle)
    whole_copy(own_slot, turn_next).wait_send()

    @pl.when(core == 0)
    def _():
        each(chunks, lambda j: image_copy(j).wait_send())

    @pl.when(core == 1)
    def _():
        per_half = TILE_ROWS // CHUNK

        def rest(j):
            @pl.when(lax.rem(j, per_half) != 0)
            def _():
                image_copy(j).wait_send()

        each(chunks, rest)


def store(image_in, text_in, loss_in, image_out, text_out, loss_out, sem):
    size = image_in.shape[0] // STORES
    loss_out[...] = loss_in[...]
    copies = []
    for i in range(STORES):
        part = pl.ds(i * size, size)
        copies.append(pltpu.make_async_copy(image_in.at[part, :], image_out.at[part, :], sem.at[2 * i]))
        copies.append(
            pltpu.make_async_copy(text_in.at[part, :], text_out.at[part, :], sem.at[2 * i + 1])
        )
    for copy in copies:
        copy.start()
    for copy in copies:
        copy.wait()


def per_device(picture_vectors, caption_vectors, sharpness_coefficient, affinity_offset):
    rows, half = picture_vectors.shape
    chunks = rows // CHUNK
    width = 2 * half
    anywhere = pl.BlockSpec(memory_space=pl.ANY)
    held = pl.BlockSpec(memory_space=pltpu.HBM)
    inside = pl.BlockSpec(memory_space=pltpu.VMEM)
    scalar = pl.BlockSpec(memory_space=pltpu.SMEM)
    dma = pltpu.SemaphoreType.DMA
    image_grad, text_grad, row_loss = pl.pallas_call(
        kernel,
        out_shape=(
            jax.ShapeDtypeStruct((half, rows), F32),
            jax.ShapeDtypeStruct((half, rows), F32),
            jax.ShapeDtypeStruct((1, rows // 2), F32),
        ),
        in_specs=[held, held, scalar, scalar],
        out_specs=(inside,) * 3,
        scratch_shapes=[
            pltpu.VMEM((width, rows), BF16),
            pltpu.VMEM((2, width, rows), BF16),
            pltpu.VMEM((width, rows), BF16),
            pltpu.VMEM((rows, width), BF16),
            pltpu.VMEM((2, width, rows), BF16),
            pltpu.VMEM((half, rows), F32),
            pltpu.VMEM((2, half, rows), F32),
            pltpu.VMEM((half, rows), BF16),
            pltpu.VMEM((half, rows), BF16),
            pltpu.VMEM((2, 8, rows), F32),
            pltpu.VMEM((8, rows), F32),
            pltpu.VMEM((rows, 128), F32),
            pltpu.VMEM((rows, 128), F32),
            pltpu.VMEM((rows, 128), F32),
            pltpu.VMEM((8, rows), F32),
            pltpu.VMEM((2, 8, rows), F32),
            dma((chunks,)),
            dma((chunks,)),
            dma((chunks,)),
            dma((chunks,)),
            dma((1,)),
            dma((1,)),
            dma((chunks,)),
            dma((chunks,)),
            dma((chunks,)),
            dma((chunks,)),
            dma((chunks,)),
            dma((chunks,)),
            dma((2,)),
            pltpu.SemaphoreType.REGULAR,
        ],
        compiler_params=pltpu.CompilerParams(
            collective_id=0, has_side_effects=True, vmem_limit_bytes=44 * 1024 * 1024
        ),
        cost_estimate=pl.CostEstimate(
            flops=8 * rows * rows * width, bytes_accessed=12 * half * rows, transcendentals=0
        ),
    )(
        pltpu.with_memory_space_constraint(picture_vectors.T, pltpu.HBM),
        pltpu.with_memory_space_constraint(caption_vectors.T, pltpu.HBM),
        sharpness_coefficient,
        affinity_offset,
    )
    image_grad, text_grad, row_loss = pl.pallas_call(
        store,
        out_shape=(
            jax.ShapeDtypeStruct((half, rows), F32),
            jax.ShapeDtypeStruct((half, rows), F32),
            jax.ShapeDtypeStruct((1, rows // 2), F32),
        ),
        in_specs=[anywhere, anywhere, inside],
        out_specs=(anywhere, anywhere, inside),
        scratch_shapes=[dma((2 * STORES,))],
        compiler_params=pltpu.CompilerParams(vmem_limit_bytes=1024 * 1024),
    )(image_grad, text_grad, row_loss)
    return image_grad.T, text_grad.T, row_loss.reshape(rows // 2)


def solution(mesh):
    placed = (P("dp", "mp"), P("dp", "mp"), P(), P())
    return jax.shard_map(
        per_device,
        mesh=mesh,
        in_specs=placed,
        out_specs=(P("dp", "mp"), P("dp", "mp"), P(("dp", "mp"))),
        check_vma=False,
    )
```

```python
import functools

import jax
import jax.numpy as jnp
from jax import lax
from jax.experimental import pallas as pl
from jax.experimental.pallas import tpu as pltpu
from jax.sharding import PartitionSpec as P

MESH = pl.DeviceIdType.MESH
F32 = jnp.float32
BF16 = jnp.bfloat16
EPSILON = 1e-06
LOG2E = 1.4426950408889634
TURN = 16
TILE_ROWS = 256
CHUNK = 256
SMALL_PARTS = 4
STORES = 4


def kernel(
    image,
    text,
    sharpness,
    offset,
    image_out,
    text_out,
    loss_out,
    image_raw,
    text_raw,
    image_unit,
    image_rows,
    text_unit,
    image_acc,
    text_acc,
    far_send,
    far_recv,
    dots,
    far_dots,
    row_dots,
    products,
    logs,
    image_inverse,
    text_inverse,
    image_ss,
    image_rs,
    text_ss,
    text_rs,
    whole_ss,
    whole_rs,
    pass_ss,
    pass_rs,
    far_ss,
    far_rs,
    dot_ss,
    dot_rs,
    local_sem,
    go_sem,
):
    half, rows = image.shape
    chunks = rows // CHUNK
    halves = rows // TILE_ROWS
    blocks = lax.axis_size("dp")
    dp = lax.axis_index("dp")
    mp = lax.axis_index("mp")
    core = lax.rem(dp, 2)
    turn_next = (lax.rem(dp, TURN) == TURN - 1).astype(jnp.int32)
    turn_prev = (lax.rem(dp, TURN) == 0).astype(jnp.int32)
    partner = (dp, 1 - mp)
    following = (lax.rem(dp + 1, blocks), mp + turn_next * (1 - 2 * mp))
    preceding = (lax.rem(dp + blocks - 1, blocks), mp + turn_prev * (1 - 2 * mp))
    own_slot = 1 - core
    prev_slot = core
    prev_offset = pl.multiple_of(turn_prev * half, half)

    def span(start, size):
        return pl.ds(pl.multiple_of(start, size), size)

    def columns(j):
        return span(j * CHUNK, CHUNK)

    def remote(src, dst, send, recv, device):
        return pltpu.make_async_remote_copy(
            src_ref=src,
            dst_ref=dst,
            send_sem=send,
            recv_sem=recv,
            device_id=device,
            device_id_type=MESH,
        )

    def image_copy(j):
        return remote(
            image.at[:, columns(j)],
            image_raw.at[pl.ds(half, half), columns(j)],
            image_ss.at[j],
            image_rs.at[j],
            partner,
        )

    def text_copy(j):
        return remote(
            text.at[:, columns(j)],
            text_raw.at[own_slot, pl.ds(half, half), columns(j)],
            text_ss.at[j],
            text_rs.at[j],
            partner,
        )

    def whole_copy(slot, turned):
        return remote(
            text,
            text_raw.at[slot, span(turned * half, half), :],
            whole_ss.at[0],
            whole_rs.at[0],
            following,
        )

    def pass_copy(slot, turned, j):
        return remote(
            text_raw.at[own_slot, pl.ds(half, half), columns(j)],
            text_raw.at[slot, span((1 - turned) * half, half), columns(j)],
            pass_ss.at[j],
            pass_rs.at[j],
            following,
        )

    def far_copy(j):
        return remote(
            far_send.at[:, columns(j)],
            far_recv.at[:, columns(j)],
            far_ss.at[j],
            far_rs.at[j],
            preceding,
        )

    def dot_copy(j):
        return remote(
            dots.at[prev_slot, :, columns(j)],
            far_dots.at[:, columns(j)],
            dot_ss.at[j],
            dot_rs.at[j],
            preceding,
        )

    def image_here():
        return pltpu.make_async_copy(image, image_raw.at[pl.ds(0, half), :], local_sem.at[0])

    def text_here():
        return pltpu.make_async_copy(
            text, text_raw.at[own_slot, pl.ds(0, half), :], local_sem.at[1]
        )

    def each(count, body):
        def step(j, carry):
            body(j)
            return carry

        lax.fori_loop(0, count, step, 0)

    scale = sharpness[0]
    slope = scale * LOG2E
    shift = offset[0] * LOG2E

    def normal(raw):
        values = raw.astype(F32)
        inverse = lax.rsqrt(jnp.sum(values * values, axis=0, keepdims=True) + EPSILON)
        return (values * inverse).astype(BF16), inverse

    def prepare_text(slot, j):
        unit, inverse = normal(text_raw[slot, :, columns(j)])
        text_unit[slot, :, columns(j)] = unit
        text_inverse[slot, 0:1, columns(j)] = inverse

    def prepare_image(j):
        unit, inverse = normal(image_raw[:, columns(j)])
        image_unit[:, columns(j)] = unit
        image_inverse[0:1, columns(j)] = inverse
        image_rows[columns(j), :] = unit.T

    def tile(slot, own, row, height, column, width, place, parts=1):
        there = pl.ds(pl.multiple_of(column, CHUNK), width)
        size = height // parts
        spans = [pl.ds(pl.multiple_of(row + i * size, size), size) for i in range(parts)]
        scores = [
            jnp.dot(image_rows[here, :], text_unit[slot, :, there], preferred_element_type=F32)
            for here in spans
        ]
        grads = []
        inner = jnp.zeros((1, width), F32)
        for i, (here, dot) in enumerate(zip(spans, scores)):
            power = dot * slope + shift
            if own:
                first = lax.broadcasted_iota(jnp.int32, dot.shape, 0) + (row + i * size - column)
                paired = first == lax.broadcasted_iota(jnp.int32, dot.shape, 1)
                power = jnp.where(paired, -power, power)
            term = jnp.exp2(power)
            total = term + 1.0
            weight = (term * scale) / total
            if own:
                weight = jnp.where(paired, -weight, weight)
            product = weight * dot
            summed, multiplied = product[:, :128], total[:, :128]
            for lane in range(128, width, 128):
                summed += product[:, lane : lane + 128]
                multiplied *= total[:, lane : lane + 128]
            row_dots[here, :] += summed
            products[here, :] *= multiplied
            inner += jnp.sum(product, axis=0, keepdims=True)
            rounded = weight.astype(BF16)
            image_acc[:, here] += lax.dot_general(
                text_unit[slot, pl.ds(0, half), there],
                rounded,
                (((1,), (1,)), ((), ())),
                preferred_element_type=F32,
            )
            grads.append(
                jnp.dot(image_unit[pl.ds(place, half), here], rounded, preferred_element_type=F32)
            )
        dots[slot, 0:1, there] += inner
        text_acc[slot, :, there] += sum(grads[1:], grads[0])

    def take_logs():
        logs[...] += jnp.log(products[...])
        products[...] = jnp.ones_like(products)

    def send_far(slot, j):
        far_send[:, columns(j)] = text_acc[slot, :, columns(j)].astype(BF16)
        far_copy(j).start()
        dot_copy(j).start()

    def finish_image():
        image_dot = jnp.sum(row_dots[...].T, axis=0, keepdims=True)
        for j in range(chunks):
            cut = slice(j * CHUNK, (j + 1) * CHUNK)
            back = image_unit[0:half, cut].astype(F32)
            image_out[:, cut] = (image_acc[:, cut] - back * image_dot[:, cut]) * image_inverse[
                0:1, cut
            ]

    def finish_loss():
        take_logs()
        image_inverse[0:1, :] = jnp.sum(logs[...].T, axis=0, keepdims=True) / (2 * rows)
        share = rows // 2
        loss_out[...] = image_inverse[0:1, span(mp * share, share)]

    def finish_text(slot, j):
        cut = columns(j)
        far_copy(j).wait_recv()
        dot_copy(j).wait_recv()
        total = text_acc[slot, :, cut] + far_recv[:, cut].astype(F32)
        dot = dots[slot, 0:1, cut] + far_dots[0:1, cut]
        back = text_unit[slot, pl.ds(0, half), cut].astype(F32)
        text_out[:, cut] = (total - back * dot) * text_inverse[slot, 0:1, cut]

    barrier = pltpu.get_barrier_semaphore()
    for device in (partner, preceding):
        pl.semaphore_signal(barrier, inc=1, device_id=device, device_id_type=MESH)
    pl.semaphore_wait(barrier, 2)

    @pl.when(core == 0)
    def _():
        each(chunks, lambda j: image_copy(j).start())

    @pl.when(core == 1)
    def _():
        each(chunks, lambda j: text_copy(j).start())
        each(chunks, lambda j: image_copy(j).start())

    whole_copy(own_slot, turn_next).start()
    image_here().start()
    text_here().start()

    image_acc[...] = jnp.zeros_like(image_acc)
    text_acc[...] = jnp.zeros_like(text_acc)
    dots[...] = jnp.zeros_like(dots)
    row_dots[...] = jnp.zeros_like(row_dots)
    logs[...] = jnp.zeros_like(logs)
    products[...] = jnp.ones_like(products)
    image_here().wait()
    text_here().wait()

    @pl.when(core == 0)
    def _():
        def arrive(j):
            image_copy(j).wait_recv()
            prepare_image(j)

        each(chunks, arrive)
        whole_copy(prev_slot, turn_prev).wait_recv()

        def first(i):
            def ready(j):
                pass_copy(prev_slot, turn_prev, 2 * i + j).wait_recv()
                prepare_text(0, 2 * i + j)

            @pl.when(i == 1)
            def _():
                pl.semaphore_wait(go_sem, 1)
                each(chunks, lambda j: text_copy(j).start())

            each(2, ready)
            tile(0, False, 0, rows, 2 * i * CHUNK, 2 * CHUNK, prev_offset)
            each(2, lambda j: send_far(0, 2 * i + j))

        each(chunks // 2, first)
        take_logs()

        def ready(j):
            text_copy(j).wait_recv()
            pass_copy(own_slot, turn_next, j).start()
            prepare_text(1, j)

        each(2, ready)
        tile(1, True, 0, rows, 0, 2 * CHUNK, 0)

        def second(j):
            ready(j + 2)
            tile(1, True, 0, rows, (j + 2) * CHUNK, CHUNK, 0, SMALL_PARTS)
            finish_text(1, j)

        each(chunks - 2, second)
        finish_image()
        finish_loss()
        each(2, lambda j: finish_text(1, chunks - 2 + j))

    @pl.when(core == 1)
    def _():
        def ready(j):
            text_copy(j).wait_recv()
            pass_copy(own_slot, turn_next, j).start()
            prepare_text(0, j)

        each(chunks, ready)
        whole_copy(prev_slot, turn_prev).wait_recv()

        per_half = TILE_ROWS // CHUNK

        def first(h):
            image_copy(h * per_half).wait_recv()
            image_copy(h * per_half).wait_send()

            @pl.when(h == 1)
            def _():
                pl.semaphore_signal(go_sem, inc=1, device_id=preceding, device_id_type=MESH)

            prepare_image(h * per_half)

            def arrive(i):
                image_copy(h * per_half + i + 1).wait_recv()
                prepare_image(h * per_half + i + 1)

            each(per_half - 1, arrive)
            each(
                2,
                lambda i: tile(0, True, h * TILE_ROWS, TILE_ROWS, 2 * i * CHUNK, 2 * CHUNK, 0),
            )

        each(halves, first)
        take_logs()

        def come(j):
            pass_copy(prev_slot, turn_prev, j).wait_recv()
            prepare_text(1, j)

        each(2, come)
        tile(1, False, 0, rows, 0, 2 * CHUNK, 0)
        each(2, lambda j: send_far(1, j))

        def second(j):
            each(2, lambda i: finish_text(0, 2 * j + i))
            come(j + 2)
            tile(1, False, 0, rows, (j + 2) * CHUNK, CHUNK, 0, SMALL_PARTS)
            send_far(1, j + 2)

        each(chunks - 2, second)
        finish_image()
        finish_loss()

    def settle(j):
        text_copy(j).wait_send()
        pass_copy(own_slot, turn_next, j).wait_send()
        far_copy(j).wait_send()
        dot_copy(j).wait_send()

    each(chunks, settle)
    whole_copy(own_slot, turn_next).wait_send()

    @pl.when(core == 0)
    def _():
        each(chunks, lambda j: image_copy(j).wait_send())

    @pl.when(core == 1)
    def _():
        per_half = TILE_ROWS // CHUNK

        def rest(j):
            @pl.when(lax.rem(j, per_half) != 0)
            def _():
                image_copy(j).wait_send()

        each(chunks, rest)


def store(image_in, text_in, loss_in, image_out, text_out, loss_out, sem):
    size = image_in.shape[0] // STORES
    loss_out[...] = loss_in[...]
    copies = []
    for i in range(STORES):
        part = pl.ds(i * size, size)
        copies.append(pltpu.make_async_copy(image_in.at[part, :], image_out.at[part, :], sem.at[2 * i]))
        copies.append(
            pltpu.make_async_copy(text_in.at[part, :], text_out.at[part, :], sem.at[2 * i + 1])
        )
    for copy in copies:
        copy.start()
    for copy in copies:
        copy.wait()


def per_device(picture_vectors, caption_vectors, sharpness_coefficient, affinity_offset):
    rows, half = picture_vectors.shape
    chunks = rows // CHUNK
    width = 2 * half
    anywhere = pl.BlockSpec(memory_space=pl.ANY)
    held = pl.BlockSpec(memory_space=pltpu.HBM)
    inside = pl.BlockSpec(memory_space=pltpu.VMEM)
    scalar = pl.BlockSpec(memory_space=pltpu.SMEM)
    dma = pltpu.SemaphoreType.DMA
    image_grad, text_grad, row_loss = pl.pallas_call(
        kernel,
        out_shape=(
            jax.ShapeDtypeStruct((half, rows), F32),
            jax.ShapeDtypeStruct((half, rows), F32),
            jax.ShapeDtypeStruct((1, rows // 2), F32),
        ),
        in_specs=[held, held, scalar, scalar],
        out_specs=(inside,) * 3,
        scratch_shapes=[
            pltpu.VMEM((width, rows), BF16),
            pltpu.VMEM((2, width, rows), BF16),
            pltpu.VMEM((width, rows), BF16),
            pltpu.VMEM((rows, width), BF16),
            pltpu.VMEM((2, width, rows), BF16),
            pltpu.VMEM((half, rows), F32),
            pltpu.VMEM((2, half, rows), F32),
            pltpu.VMEM((half, rows), BF16),
            pltpu.VMEM((half, rows), BF16),
            pltpu.VMEM((2, 8, rows), F32),
            pltpu.VMEM((8, rows), F32),
            pltpu.VMEM((rows, 128), F32),
            pltpu.VMEM((rows, 128), F32),
            pltpu.VMEM((rows, 128), F32),
            pltpu.VMEM((8, rows), F32),
            pltpu.VMEM((2, 8, rows), F32),
            dma((chunks,)),
            dma((chunks,)),
            dma((chunks,)),
            dma((chunks,)),
            dma((1,)),
            dma((1,)),
            dma((chunks,)),
            dma((chunks,)),
            dma((chunks,)),
            dma((chunks,)),
            dma((chunks,)),
            dma((chunks,)),
            dma((2,)),
            pltpu.SemaphoreType.REGULAR,
        ],
        compiler_params=pltpu.CompilerParams(
            collective_id=0, has_side_effects=True, vmem_limit_bytes=44 * 1024 * 1024
        ),
        cost_estimate=pl.CostEstimate(
            flops=8 * rows * rows * width, bytes_accessed=12 * half * rows, transcendentals=0
        ),
    )(
        pltpu.with_memory_space_constraint(picture_vectors.T, pltpu.HBM),
        pltpu.with_memory_space_constraint(caption_vectors.T, pltpu.HBM),
        sharpness_coefficient,
        affinity_offset,
    )
    image_grad, text_grad, row_loss = pl.pallas_call(
        store,
        out_shape=(
            jax.ShapeDtypeStruct((half, rows), F32),
            jax.ShapeDtypeStruct((half, rows), F32),
            jax.ShapeDtypeStruct((1, rows // 2), F32),
        ),
        in_specs=[anywhere, anywhere, inside],
        out_specs=(anywhere, anywhere, inside),
        scratch_shapes=[dma((2 * STORES,))],
        compiler_params=pltpu.CompilerParams(vmem_limit_bytes=1024 * 1024),
    )(image_grad, text_grad, row_loss)
    return image_grad.T, text_grad.T, row_loss.reshape(rows // 2)


def solution(mesh):
    placed = (P("dp", "mp"), P("dp", "mp"), P(), P())
    return jax.shard_map(
        per_device,
        mesh=mesh,
        in_specs=placed,
        out_specs=(P("dp", "mp"), P("dp", "mp"), P(("dp", "mp"))),
        check_vma=False,
    )
```

```python
import functools

import jax
import jax.numpy as jnp
from jax import lax
from jax.experimental import pallas as pl
from jax.experimental.pallas import tpu as pltpu
from jax.sharding import PartitionSpec as P

MESH = pl.DeviceIdType.MESH
F32 = jnp.float32
BF16 = jnp.bfloat16
EPSILON = 1e-06
LOG2E = 1.4426950408889634
TURN = 16
TILE_ROWS = 256
CHUNK = 256
SMALL_PARTS = 4
STORES = 1


def kernel(
    image,
    text,
    sharpness,
    offset,
    image_out,
    text_out,
    loss_out,
    image_raw,
    text_raw,
    image_unit,
    image_rows,
    text_unit,
    image_acc,
    text_acc,
    far_send,
    far_recv,
    dots,
    far_dots,
    row_dots,
    products,
    logs,
    image_inverse,
    text_inverse,
    image_ss,
    image_rs,
    text_ss,
    text_rs,
    whole_ss,
    whole_rs,
    pass_ss,
    pass_rs,
    far_ss,
    far_rs,
    dot_ss,
    dot_rs,
    local_sem,
    go_sem,
):
    half, rows = image.shape
    chunks = rows // CHUNK
    halves = rows // TILE_ROWS
    blocks = lax.axis_size("dp")
    dp = lax.axis_index("dp")
    mp = lax.axis_index("mp")
    core = lax.rem(dp, 2)
    turn_next = (lax.rem(dp, TURN) == TURN - 1).astype(jnp.int32)
    turn_prev = (lax.rem(dp, TURN) == 0).astype(jnp.int32)
    partner = (dp, 1 - mp)
    following = (lax.rem(dp + 1, blocks), mp + turn_next * (1 - 2 * mp))
    preceding = (lax.rem(dp + blocks - 1, blocks), mp + turn_prev * (1 - 2 * mp))
    own_slot = 1 - core
    prev_slot = core
    prev_offset = pl.multiple_of(turn_prev * half, half)

    def span(start, size):
        return pl.ds(pl.multiple_of(start, size), size)

    def columns(j):
        return span(j * CHUNK, CHUNK)

    def remote(src, dst, send, recv, device):
        return pltpu.make_async_remote_copy(
            src_ref=src,
            dst_ref=dst,
            send_sem=send,
            recv_sem=recv,
            device_id=device,
            device_id_type=MESH,
        )

    def image_copy(j):
        return remote(
            image.at[:, columns(j)],
            image_raw.at[pl.ds(half, half), columns(j)],
            image_ss.at[j],
            image_rs.at[j],
            partner,
        )

    def text_copy(j):
        return remote(
            text.at[:, columns(j)],
            text_raw.at[own_slot, pl.ds(half, half), columns(j)],
            text_ss.at[j],
            text_rs.at[j],
            partner,
        )

    def whole_copy(slot, turned):
        return remote(
            text,
            text_raw.at[slot, span(turned * half, half), :],
            whole_ss.at[0],
            whole_rs.at[0],
            following,
        )

    def pass_copy(slot, turned, j):
        return remote(
            text_raw.at[own_slot, pl.ds(half, half), columns(j)],
            text_raw.at[slot, span((1 - turned) * half, half), columns(j)],
            pass_ss.at[j],
            pass_rs.at[j],
            following,
        )

    def far_copy(j):
        return remote(
            far_send.at[:, columns(j)],
            far_recv.at[:, columns(j)],
            far_ss.at[j],
            far_rs.at[j],
            preceding,
        )

    def dot_copy(j):
        return remote(
            dots.at[prev_slot, :, columns(j)],
            far_dots.at[:, columns(j)],
            dot_ss.at[j],
            dot_rs.at[j],
            preceding,
        )

    def image_here():
        return pltpu.make_async_copy(image, image_raw.at[pl.ds(0, half), :], local_sem.at[0])

    def text_here():
        return pltpu.make_async_copy(
            text, text_raw.at[own_slot, pl.ds(0, half), :], local_sem.at[1]
        )

    def each(count, body):
        def step(j, carry):
            body(j)
            return carry

        lax.fori_loop(0, count, step, 0)

    scale = sharpness[0]
    slope = scale * LOG2E
    shift = offset[0] * LOG2E

    def normal(raw):
        values = raw.astype(F32)
        inverse = lax.rsqrt(jnp.sum(values * values, axis=0, keepdims=True) + EPSILON)
        return (values * inverse).astype(BF16), inverse

    def prepare_text(slot, j):
        unit, inverse = normal(text_raw[slot, :, columns(j)])
        text_unit[slot, :, columns(j)] = unit
        text_inverse[slot, 0:1, columns(j)] = inverse

    def prepare_image(j):
        unit, inverse = normal(image_raw[:, columns(j)])
        image_unit[:, columns(j)] = unit
        image_inverse[0:1, columns(j)] = inverse
        image_rows[columns(j), :] = unit.T

    def tile(slot, own, row, height, column, width, place, parts=1):
        there = pl.ds(pl.multiple_of(column, CHUNK), width)
        size = height // parts
        spans = [pl.ds(pl.multiple_of(row + i * size, size), size) for i in range(parts)]
        scores = [
            jnp.dot(image_rows[here, :], text_unit[slot, :, there], preferred_element_type=F32)
            for here in spans
        ]
        grads = []
        inner = jnp.zeros((1, width), F32)
        for i, (here, dot) in enumerate(zip(spans, scores)):
            power = dot * slope + shift
            if own:
                first = lax.broadcasted_iota(jnp.int32, dot.shape, 0) + (row + i * size - column)
                paired = first == lax.broadcasted_iota(jnp.int32, dot.shape, 1)
                power = jnp.where(paired, -power, power)
            term = jnp.exp2(power)
            total = term + 1.0
            weight = (term * scale) / total
            if own:
                weight = jnp.where(paired, -weight, weight)
            product = weight * dot
            summed, multiplied = product[:, :128], total[:, :128]
            for lane in range(128, width, 128):
                summed += product[:, lane : lane + 128]
                multiplied *= total[:, lane : lane + 128]
            row_dots[here, :] += summed
            products[here, :] *= multiplied
            inner += jnp.sum(product, axis=0, keepdims=True)
            rounded = weight.astype(BF16)
            image_acc[:, here] += lax.dot_general(
                text_unit[slot, pl.ds(0, half), there],
                rounded,
                (((1,), (1,)), ((), ())),
                preferred_element_type=F32,
            )
            grads.append(
                jnp.dot(image_unit[pl.ds(place, half), here], rounded, preferred_element_type=F32)
            )
        dots[slot, 0:1, there] += inner
        text_acc[slot, :, there] += sum(grads[1:], grads[0])

    def take_logs():
        logs[...] += jnp.log(products[...])
        products[...] = jnp.ones_like(products)

    def send_far(slot, j):
        far_send[:, columns(j)] = text_acc[slot, :, columns(j)].astype(BF16)
        far_copy(j).start()
        dot_copy(j).start()

    def finish_image():
        image_dot = jnp.sum(row_dots[...].T, axis=0, keepdims=True)
        for j in range(chunks):
            cut = slice(j * CHUNK, (j + 1) * CHUNK)
            back = image_unit[0:half, cut].astype(F32)
            image_out[:, cut] = (image_acc[:, cut] - back * image_dot[:, cut]) * image_inverse[
                0:1, cut
            ]

    def finish_loss():
        take_logs()
        image_inverse[0:1, :] = jnp.sum(logs[...].T, axis=0, keepdims=True) / (2 * rows)
        share = rows // 2
        loss_out[...] = image_inverse[0:1, span(mp * share, share)]

    def finish_text(slot, j):
        cut = columns(j)
        far_copy(j).wait_recv()
        dot_copy(j).wait_recv()
        total = text_acc[slot, :, cut] + far_recv[:, cut].astype(F32)
        dot = dots[slot, 0:1, cut] + far_dots[0:1, cut]
        back = text_unit[slot, pl.ds(0, half), cut].astype(F32)
        text_out[:, cut] = (total - back * dot) * text_inverse[slot, 0:1, cut]

    barrier = pltpu.get_barrier_semaphore()
    for device in (partner, preceding):
        pl.semaphore_signal(barrier, inc=1, device_id=device, device_id_type=MESH)
    pl.semaphore_wait(barrier, 2)

    @pl.when(core == 0)
    def _():
        each(chunks, lambda j: image_copy(j).start())

    @pl.when(core == 1)
    def _():
        each(chunks, lambda j: text_copy(j).start())
        each(chunks, lambda j: image_copy(j).start())

    whole_copy(own_slot, turn_next).start()
    image_here().start()
    text_here().start()

    image_acc[...] = jnp.zeros_like(image_acc)
    text_acc[...] = jnp.zeros_like(text_acc)
    dots[...] = jnp.zeros_like(dots)
    row_dots[...] = jnp.zeros_like(row_dots)
    logs[...] = jnp.zeros_like(logs)
    products[...] = jnp.ones_like(products)
    image_here().wait()
    text_here().wait()

    @pl.when(core == 0)
    def _():
        def arrive(j):
            image_copy(j).wait_recv()
            prepare_image(j)

        each(chunks, arrive)
        whole_copy(prev_slot, turn_prev).wait_recv()

        def first(i):
            def ready(j):
                pass_copy(prev_slot, turn_prev, 2 * i + j).wait_recv()
                prepare_text(0, 2 * i + j)

            @pl.when(i == 1)
            def _():
                pl.semaphore_wait(go_sem, 1)
                each(chunks, lambda j: text_copy(j).start())

            each(2, ready)
            tile(0, False, 0, rows, 2 * i * CHUNK, 2 * CHUNK, prev_offset)
            each(2, lambda j: send_far(0, 2 * i + j))

        each(chunks // 2, first)
        take_logs()

        def ready(j):
            text_copy(j).wait_recv()
            pass_copy(own_slot, turn_next, j).start()
            prepare_text(1, j)

        each(2, ready)
        tile(1, True, 0, rows, 0, 2 * CHUNK, 0)

        def second(j):
            ready(j + 2)
            tile(1, True, 0, rows, (j + 2) * CHUNK, CHUNK, 0, SMALL_PARTS)
            finish_text(1, j)

        each(chunks - 2, second)
        finish_image()
        finish_loss()
        each(2, lambda j: finish_text(1, chunks - 2 + j))

    @pl.when(core == 1)
    def _():
        def ready(j):
            text_copy(j).wait_recv()
            pass_copy(own_slot, turn_next, j).start()
            prepare_text(0, j)

        each(chunks, ready)
        whole_copy(prev_slot, turn_prev).wait_recv()

        per_half = TILE_ROWS // CHUNK

        def first(h):
            image_copy(h * per_half).wait_recv()
            image_copy(h * per_half).wait_send()

            @pl.when(h == 1)
            def _():
                pl.semaphore_signal(go_sem, inc=1, device_id=preceding, device_id_type=MESH)

            prepare_image(h * per_half)

            def arrive(i):
                image_copy(h * per_half + i + 1).wait_recv()
                prepare_image(h * per_half + i + 1)

            each(per_half - 1, arrive)
            each(
                2,
                lambda i: tile(0, True, h * TILE_ROWS, TILE_ROWS, 2 * i * CHUNK, 2 * CHUNK, 0),
            )

        each(halves, first)
        take_logs()

        def come(j):
            pass_copy(prev_slot, turn_prev, j).wait_recv()
            prepare_text(1, j)

        each(2, come)
        tile(1, False, 0, rows, 0, 2 * CHUNK, 0)
        each(2, lambda j: send_far(1, j))

        def second(j):
            each(2, lambda i: finish_text(0, 2 * j + i))
            come(j + 2)
            tile(1, False, 0, rows, (j + 2) * CHUNK, CHUNK, 0, SMALL_PARTS)
            send_far(1, j + 2)

        each(chunks - 2, second)
        finish_image()
        finish_loss()

    def settle(j):
        text_copy(j).wait_send()
        pass_copy(own_slot, turn_next, j).wait_send()
        far_copy(j).wait_send()
        dot_copy(j).wait_send()

    each(chunks, settle)
    whole_copy(own_slot, turn_next).wait_send()

    @pl.when(core == 0)
    def _():
        each(chunks, lambda j: image_copy(j).wait_send())

    @pl.when(core == 1)
    def _():
        per_half = TILE_ROWS // CHUNK

        def rest(j):
            @pl.when(lax.rem(j, per_half) != 0)
            def _():
                image_copy(j).wait_send()

        each(chunks, rest)


def store(image_in, text_in, loss_in, image_out, text_out, loss_out, sem):
    size = image_in.shape[0] // STORES
    loss_out[...] = loss_in[...]
    copies = []
    for i in range(STORES):
        part = pl.ds(i * size, size)
        copies.append(pltpu.make_async_copy(image_in.at[part, :], image_out.at[part, :], sem.at[2 * i]))
        copies.append(
            pltpu.make_async_copy(text_in.at[part, :], text_out.at[part, :], sem.at[2 * i + 1])
        )
    for copy in copies:
        copy.start()
    for copy in copies:
        copy.wait()


def per_device(picture_vectors, caption_vectors, sharpness_coefficient, affinity_offset):
    rows, half = picture_vectors.shape
    chunks = rows // CHUNK
    width = 2 * half
    anywhere = pl.BlockSpec(memory_space=pl.ANY)
    held = pl.BlockSpec(memory_space=pltpu.HBM)
    inside = pl.BlockSpec(memory_space=pltpu.VMEM)
    scalar = pl.BlockSpec(memory_space=pltpu.SMEM)
    dma = pltpu.SemaphoreType.DMA
    image_grad, text_grad, row_loss = pl.pallas_call(
        kernel,
        out_shape=(
            jax.ShapeDtypeStruct((half, rows), F32),
            jax.ShapeDtypeStruct((half, rows), F32),
            jax.ShapeDtypeStruct((1, rows // 2), F32),
        ),
        in_specs=[held, held, scalar, scalar],
        out_specs=(inside,) * 3,
        scratch_shapes=[
            pltpu.VMEM((width, rows), BF16),
            pltpu.VMEM((2, width, rows), BF16),
            pltpu.VMEM((width, rows), BF16),
            pltpu.VMEM((rows, width), BF16),
            pltpu.VMEM((2, width, rows), BF16),
            pltpu.VMEM((half, rows), F32),
            pltpu.VMEM((2, half, rows), F32),
            pltpu.VMEM((half, rows), BF16),
            pltpu.VMEM((half, rows), BF16),
            pltpu.VMEM((2, 8, rows), F32),
            pltpu.VMEM((8, rows), F32),
            pltpu.VMEM((rows, 128), F32),
            pltpu.VMEM((rows, 128), F32),
            pltpu.VMEM((rows, 128), F32),
            pltpu.VMEM((8, rows), F32),
            pltpu.VMEM((2, 8, rows), F32),
            dma((chunks,)),
            dma((chunks,)),
            dma((chunks,)),
            dma((chunks,)),
            dma((1,)),
            dma((1,)),
            dma((chunks,)),
            dma((chunks,)),
            dma((chunks,)),
            dma((chunks,)),
            dma((chunks,)),
            dma((chunks,)),
            dma((2,)),
            pltpu.SemaphoreType.REGULAR,
        ],
        compiler_params=pltpu.CompilerParams(
            collective_id=0, has_side_effects=True, vmem_limit_bytes=44 * 1024 * 1024
        ),
        cost_estimate=pl.CostEstimate(
            flops=8 * rows * rows * width, bytes_accessed=12 * half * rows, transcendentals=0
        ),
    )(
        pltpu.with_memory_space_constraint(picture_vectors.T, pltpu.HBM),
        pltpu.with_memory_space_constraint(caption_vectors.T, pltpu.HBM),
        sharpness_coefficient,
        affinity_offset,
    )
    image_grad, text_grad, row_loss = pl.pallas_call(
        store,
        out_shape=(
            jax.ShapeDtypeStruct((half, rows), F32),
            jax.ShapeDtypeStruct((half, rows), F32),
            jax.ShapeDtypeStruct((1, rows // 2), F32),
        ),
        in_specs=[anywhere, anywhere, inside],
        out_specs=(anywhere, anywhere, inside),
        scratch_shapes=[dma((2 * STORES,))],
        compiler_params=pltpu.CompilerParams(vmem_limit_bytes=1024 * 1024),
    )(image_grad, text_grad, row_loss)
    return image_grad.T, text_grad.T, row_loss.reshape(rows // 2)


def solution(mesh):
    placed = (P("dp", "mp"), P("dp", "mp"), P(), P())
    return jax.shard_map(
        per_device,
        mesh=mesh,
        in_specs=placed,
        out_specs=(P("dp", "mp"), P("dp", "mp"), P(("dp", "mp"))),
        check_vma=False,
    )
```
